512 devices in a mesh: dp: 8 (over z), expert: 64 (over y, x, core).
Axes of the slice: x: 4, y: 8, z: 8, core: 2. Of those that a mesh axis runs over, the one named last changes fastest.
Arguments:
- tokens: bfloat16 [65536, 2048], P(('dp', 'expert')), may hold values from -24 to 24
- latent_grad: bfloat16 [65536, 512], P(('dp', 'expert')), may hold values from -6 to 6
- routes: int32 [65536, 8], P(('dp', 'expert')), may hold values from 0 to 63, all different within a row; in each aligned block of 128 rows (0 to 127, 128 to 255, ...) at most 24 rows name the same one
- route_weights: bfloat16 [65536, 8], P(('dp', 'expert')), may hold values from 0.099609375 to 1
- down_proj: bfloat16 [2048, 512], P(('dp', 'expert')), may hold values from -0.125 to 0.125
- expert_up: bfloat16 [64, 512, 1024], P('expert'), may hold values from -0.25 to 0.25
- expert_down: bfloat16 [64, 1024, 512], P('expert'), may hold values from -0.1875 to 0.1875
Outputs:
- input_grad: bfloat16 [65536, 2048], P(('dp', 'expert'))
- proj_grad: float32 [2048, 512], P(('dp', 'expert'))
- weight_grad: bfloat16 [65536, 8], P(('dp', 'expert'))
The draws below stay inside these ranges and needn't reach their ends.
Inputs may be any that keep to these rules, and one draw needn't show every extreme that they name: `routes`: each row names 8 different experts. Within the rows of one device (aligned blocks of 128 rows) no expert is named by more than 24 rows, a bound that some block reaches; every expert is named somewhere.
All inputs are finite; a program needn't handle non-finite values.
Results may differ from the reference program's by a relative error of at most 0.009.
Values may be sent and summed in bfloat16 or wider, within the bound.
A program may use at most 64 MiB of HBM per device.

```python
import math
import jax
import jax.numpy as jnp
import numpy as np
from jax import lax

D = 2048
LAT = 512
HID = 1024
TOP = 8
TOK_DEV = 128
EXPERTS = 64
CAP = 24
TOKENS = 65536
N_DP = 8
N_EXPERT = 64


def spiked(drawn, rng, source, target, shards_of, factor):
    owner, partner = [(jnp.arange(drawn.shape[position]) // (drawn.shape[position] // shards_of)).reshape([-1 if axis == position else 1 for axis in range(drawn.ndim)]) for position in (source, target)]
    chosen = jax.random.permutation(rng, shards_of)[partner]
    strong = (owner == chosen) | (owner == (partner + shards_of // 2) % shards_of)
    return jnp.where(strong, factor * drawn, drawn)


def block_levels(stream_key, shape, cuts, smallest, high):
    loudness, own = 1.0, jax.random.fold_in(stream_key, 6)
    for axis_at, shards_of in cuts:
        heights = jnp.exp(jax.random.uniform(jax.random.fold_in(own, axis_at), (shards_of,), jnp.float32, smallest / len(cuts), high / len(cuts)))
        loudness = loudness * jnp.repeat(heights, shape[axis_at] // shards_of).reshape([-1 if axis == axis_at else 1 for axis in range(len(shape))])
    return loudness


def shared_out(own_key, own, number, rows, count, top, most, lean):
    sequence = jax.random.permutation(own_key, count)
    heavy_load, ordinary = load_shares(count, rows * top, most, lean, True), load_shares(count, rows * top, most, lean, False)
    places = jnp.arange(count)

    def named(lengths, offset_by):
        used = int((lengths > 0).sum())
        fixed = max(1, used // 4)
        moved = fixed + (places - fixed + offset_by * (used - fixed)) % max(1, count - fixed)
        return jnp.zeros((count,), jnp.int32).at[sequence[jnp.where(places < fixed, places, moved)]].set(jnp.asarray(lengths, jnp.int32))

    lengths = jnp.where(number % 4 == 0, named(heavy_load, number // 4), named(ordinary, number - number // 4 - 1))
    mixed = jax.random.permutation(jax.random.fold_in(own, 3), count)
    source_of, sink = mixed[0:count // 2 * 2:2], mixed[1:count // 2 * 2:2]
    margin = jnp.minimum(lengths[source_of] - 1, most - lengths[sink]) // 2
    margin = jnp.where((source_of == sequence[0]) | (sink == sequence[0]) | (lengths[sink] == 0), 0, jnp.maximum(margin, 0))
    moved = jax.random.randint(jax.random.fold_in(own, 4), (count // 2,), 0, 1 << 20) % (margin + 1)
    lengths = lengths.at[source_of].add(-moved).at[sink].add(moved)
    items = jnp.searchsorted(jnp.cumsum(lengths), jnp.arange(rows * top), side="right").astype(jnp.int32)
    listing = items.reshape(top, rows).T
    listing = listing[jax.random.permutation(jax.random.fold_in(own, 1), rows)]
    offset_by = jax.random.randint(jax.random.fold_in(own, 2), (rows, 1), 0, top)
    return jnp.take_along_axis(listing, (jnp.arange(top)[None, :] + offset_by) % top, axis=1)


def load_shares(number_of, total, reach, skew, full):
    portions = [(1 << 20) // math.isqrt(standing ** skew) + 1 for standing in range(1, number_of + 1)]
    largest = reach if full else min(reach, max(-(-total // number_of), total * portions[0] // sum(portions)))
    least = 1 if total - largest >= number_of - 1 else 0
    given, rest = [largest] + [least] * (number_of - 1), total - largest - least * (number_of - 1)
    while rest > 0:
        movable = [i for i in range(1, number_of) if given[i] < largest] or [i for i in range(1, number_of) if given[i] < reach]
        pool, left = sum([portions[i] for i in movable]), rest
        for i in movable:
            addition = min(reach - given[i], max(1, left * portions[i] // pool), rest)
            given[i] = given[i] + addition
            rest = rest - addition
    return np.array(given)


def noise(own_key, shape, deviation, most, cuts=(), kind=jnp.bfloat16):
    drawn = jax.random.normal(own_key, shape, jnp.float32) * deviation
    if len(cuts) > 0:
        drawn = block_levels(own_key, shape, cuts, -0.22, 0.18) * drawn
    return jnp.clip(drawn, min=-most, max=most).astype(kind)


def heavy_noise(rng, extent, width, most, shards, heavy, kind=jnp.bfloat16):
    array = width * jax.random.normal(rng, extent, jnp.float32)
    if shards:
        array = array * block_levels(rng, extent, shards, -0.22, 0.18)
    return jnp.clip(spiked(array, jax.random.fold_in(rng, 3), *heavy), -most, most).astype(kind)


def setup_inputs(seed: int = 0) -> dict:
    arg_keys = jax.random.split(jax.random.key(seed), 8)
    tokens = heavy_noise(arg_keys[0], (TOKENS, D), 1.0, 24.0, ((0, 512),), (0, 1, 512, 6.0))
    latent_grad = noise(arg_keys[1], (TOKENS, LAT), 1.0, 6.0, ((0, 512),))
    routes_keys = jax.random.split(jax.random.fold_in(arg_keys[2], 1), TOKENS // TOK_DEV)
    routes_turns = jax.random.permutation(jax.random.fold_in(arg_keys[2], 3), TOKENS // TOK_DEV)
    routes = jax.vmap(lambda own, number: shared_out(jax.random.fold_in(arg_keys[2], 2), own, number, TOK_DEV, EXPERTS, TOP, CAP, 2))(routes_keys, routes_turns).reshape((TOKENS, TOP))
    route_weights = jnp.clip(0.099609375 + 0.9003906 * jax.random.uniform(arg_keys[3], (TOKENS, TOP), jnp.float32) ** block_levels(arg_keys[3], (TOKENS, TOP), ((0, 512),), -0.2, 0.2), 0.099609375, 1.0).astype(jnp.bfloat16)
    down_proj = noise(arg_keys[4], (D, LAT), D ** -0.5, 0.125, ((0, 512),))
    expert_up = noise(arg_keys[5], (EXPERTS, LAT, HID), LAT ** -0.5, 0.25, ((0, 64),))
    expert_down = noise(arg_keys[6], (EXPERTS, HID, LAT), HID ** -0.5, 0.1875, ((0, 64),))
    return {"tokens": tokens, "latent_grad": latent_grad, "routes": routes, "route_weights": route_weights, "down_proj": down_proj, "expert_up": expert_up, "expert_down": expert_down}


def reference(tokens, latent_grad, routes, route_weights, down_proj, expert_up, expert_down):
    latent = jnp.dot(tokens, down_proj, preferred_element_type=jnp.float32).astype(jnp.bfloat16)
    flat_ids = routes.reshape(-1).astype(jnp.int32)
    slots_all = flat_ids.shape[0]
    owner_row = jnp.arange(slots_all, dtype=jnp.int32) // TOP
    owner_ext = jnp.concatenate([owner_row, jnp.full((1,), TOKENS, jnp.int32)])
    latent_ext = jnp.concatenate([latent, jnp.zeros((1, LAT), latent.dtype)])
    grad_ext = jnp.concatenate([latent_grad, jnp.zeros((1, LAT), latent_grad.dtype)])
    weight_ext = jnp.concatenate([route_weights.reshape(-1).astype(jnp.float32), jnp.zeros((1,), jnp.float32)])
    max_rows = N_DP * N_EXPERT * CAP

    def one_expert(state_pair, expert_id):
        summed, weight_grad = state_pair
        picked = jnp.nonzero(flat_ids == expert_id, size=max_rows, fill_value=slots_all)[0].astype(jnp.int32)
        token_index = owner_ext[picked]
        up_matrix = lax.dynamic_index_in_dim(expert_up, expert_id, 0, keepdims=False)
        down_matrix = lax.dynamic_index_in_dim(expert_down, expert_id, 0, keepdims=False)
        pre_act = jnp.dot(latent_ext[token_index], up_matrix, preferred_element_type=jnp.float32)
        back_grad = lax.dot_general(grad_ext[token_index], down_matrix, (((1,), (1,)), ((), ())), preferred_element_type=jnp.float32)
        active = jnp.maximum(pre_act, 0.0)
        weight_part = jnp.sum(back_grad * active * active, axis=1).astype(jnp.bfloat16)
        pre_grad = (weight_ext[picked][:, None] * back_grad * (2.0 * active)).astype(jnp.bfloat16)
        row_grad = lax.dot_general(pre_grad, up_matrix, (((1,), (1,)), ((), ())), preferred_element_type=jnp.float32).astype(jnp.bfloat16)
        summed = summed.at[token_index].add(row_grad.astype(jnp.float32), mode="drop")
        weight_grad = weight_grad.at[picked].set(weight_part, mode="drop")
        return (summed, weight_grad), None

    start_pair = (jnp.zeros((TOKENS, LAT), jnp.float32), jnp.zeros((slots_all,), jnp.bfloat16))
    (summed, weight_grad), unused = lax.scan(one_expert, start_pair, jnp.arange(EXPERTS, dtype=jnp.int32))
    latent_sum = summed.astype(jnp.bfloat16)
    input_grad = lax.dot_general(latent_sum, down_proj, (((1,), (1,)), ((), ())), preferred_element_type=jnp.float32).astype(jnp.bfloat16)
    proj_grad = lax.dot_general(tokens, latent_sum, (((0,), (0,)), ((), ())), preferred_element_type=jnp.float32)
    return input_grad, proj_grad, weight_grad.reshape(TOKENS, TOP)
```

```python
import functools

import jax
import jax.numpy as jnp
from jax import lax
from jax.experimental import pallas as pl
from jax.experimental.pallas import tpu as pltpu
from jax.sharding import PartitionSpec as P

MESH = pl.DeviceIdType.MESH
BF = jnp.bfloat16
F32 = jnp.float32
NC = 2


def xor(a, b, n):
    total, bit = 0, 1
    while bit < n:
        total = total + ((a // bit) % 2 + (b // bit) % 2) % 2 * bit
        bit *= 2
    return total


def nt_dot(a, b):
    return lax.dot_general(a, b, (((1,), (1,)), ((), ())), preferred_element_type=F32)


def dot(a, b):
    return jnp.dot(a, b, preferred_element_type=F32)


def remote(src, dst, sems, at, device):
    return pltpu.make_async_remote_copy(
        src_ref=src,
        dst_ref=dst,
        send_sem=sems.at[(0, *at)],
        recv_sem=sems.at[(1, *at)],
        device_id=device,
        device_id_type=MESH,
    )


def kernel(
    sizes,
    tokens, grad, routes_t, weights_t, own_rows, up, down,
    input_grad, proj_grad, weight_grad,
    proj, padded, meta, g_all, l_all, pick, back, g_send, l_send, g_got, l_got, bg,
    r_send, r_got, v_send, v_got, p_send, p_got, q_send, q_got,
    tok_far, tok_t, lsum, lsum_far, pg32, pg16, x_got, s32, s16, y_got, t16, z_got, f_send, f_got,
    sem_a, sem_b, sem_c, sem_d, sem_m, sem_g, sem_l, sem_gx, sem_lx, sem_r, sem_v, sem_p, sem_q,
    sem_tok, sem_ls, sem_x, sem_y, sem_z, sem_f,
):
    nz, ny, nx, cap = sizes
    g8 = nx * NC
    halves = nx // 2
    pairs = ny // 2
    toks = tokens.shape[0]
    lat = grad.shape[1]
    hid = up.shape[1]
    z = lax.axis_index("dp")
    e = lax.axis_index("expert")
    y = e // g8
    me8 = e % g8
    x, c = me8 // NC, me8 % NC

    def dev_z(o):
        return (xor(z, o, nz), e)

    def dev_y(o):
        return (z, xor(y, o, ny) * g8 + me8)

    def dev_8(o):
        return (z, y * g8 + xor(me8, o, g8))

    def share_of(m8):
        mx, mc = m8 // NC, m8 % NC
        return mx // 2, pl.multiple_of((mc * 2 + mx % 2) * 128, 128)

    barrier = pltpu.get_barrier_semaphore()
    for o in range(1, nz):
        pl.semaphore_signal(barrier, inc=1, device_id=dev_z(o), device_id_type=MESH)
    for o in range(1, ny):
        pl.semaphore_signal(barrier, inc=1, device_id=dev_y(o), device_id_type=MESH)
    for o in range(1, g8):
        pl.semaphore_signal(barrier, inc=1, device_id=dev_8(o), device_id_type=MESH)
    pl.semaphore_wait(barrier, nz + ny + g8 - 3)

    half, lane = share_of(me8)
    zy = z * ny + y
    sends = []

    def a_copy(o):
        _, far_lane = share_of(xor(me8, o, g8))
        return remote(own_rows.at[:, pl.ds(far_lane, 128)], padded.at[o], sem_a, (o,), dev_8(o))

    for o in range(1, 4):
        cp = a_copy(o)
        cp.start()
        sends.append(cp)

    row = lax.broadcasted_iota(jnp.int32, (ny * g8, toks), 0)
    expert = ((row // g8) ^ y) * g8 + ((row % g8) ^ me8)
    named = jnp.zeros((ny * g8, toks), F32)
    weight = jnp.zeros((ny * g8, toks), F32)
    for k in range(routes_t.shape[0]):
        hit = routes_t[k : k + 1, :] == expert
        named = jnp.where(hit, 1.0, named)
        weight = jnp.where(hit, weights_t[k : k + 1, :], weight)
    earlier = (
        lax.broadcasted_iota(jnp.int32, (toks, toks), 0)
        < lax.broadcasted_iota(jnp.int32, (toks, toks), 1)
    )
    rank = dot(named.astype(BF), jnp.where(earlier, 1.0, 0.0).astype(BF))
    rank = jnp.where(named > 0.5, rank, -1.0)
    meta[0] = jnp.concatenate(
        [rank.reshape(ny, g8, toks), weight.reshape(ny, g8, toks)], axis=1
    )

    own = own_rows[:, pl.ds(lane, 128)].astype(F32)
    for o in range(1, 4):
        a_copy(o).wait_recv()
        own = own + padded[o].astype(F32)
    proj[zy, half, :, pl.ds(lane, 128)] = own.astype(BF)

    def b_copy(o, at):
        ref = proj.at[at, half, :, pl.ds(lane, 128)]
        return remote(ref, ref, sem_b, (o,), dev_y(o))

    for o in range(1, ny):
        cp = b_copy(o, zy)
        cp.start()
        sends.append(cp)

    g_all[0] = grad[...]

    def m_copy(o):
        return remote(meta.at[0, o], meta.at[1, o], sem_m, (o,), dev_y(o))

    def g_copy(o):
        return remote(grad, g_all.at[o], sem_g, (o,), dev_y(o))

    meta[1, 0] = meta[0, 0]
    for o in range(1, ny):
        for cp in (m_copy(o), g_copy(o)):
            cp.start()
            sends.append(cp)
    tok_copy = remote(tokens, tok_far, sem_tok, (0,), dev_8(1))
    tok_copy.start()
    sends.append(tok_copy)

    for o in range(1, ny):
        b_copy(o, z * ny + xor(y, o, ny)).wait_recv()

    def c_copy(o, at_z):
        ref = proj.at[pl.ds(at_z * ny, ny), half, :, pl.ds(lane, 128)]
        return remote(ref, ref, sem_c, (o,), dev_z(o))

    for o in range(1, nz):
        cp = c_copy(o, z)
        cp.start()
        sends.append(cp)

    tok_copy.wait_recv()
    step = min(256, tokens.shape[1])

    @pl.loop(0, tokens.shape[1] // step)
    def _(n):
        at = pl.ds(pl.multiple_of(n * step, step), step)
        both = jnp.concatenate([tokens[:, at], tok_far[:, at]], axis=0)
        tok_t[at, :] = both.astype(F32).T.astype(BF)

    for o in range(1, nz):
        c_copy(o, xor(z, o, nz)).wait_recv()

    def d_copy(o, share, to):
        h, l = share_of(share)
        ref = proj.at[:, h, :, pl.ds(l, 128)]
        return remote(ref, ref, sem_d, (o,), dev_8(to))

    for o in range(2, g8, 2):
        cp = d_copy(o, me8, o)
        cp.start()
        sends.append(cp)
    cp = d_copy(1, me8, 1)
    cp.start()
    sends.append(cp)

    place = lax.broadcasted_iota(jnp.int32, (cap, toks), 0).astype(F32)

    def wait_y(copy, i):
        @pl.when(i > 0)
        def _():
            copy(2 * i).wait_recv()

        copy(2 * i + 1).wait_recv()

    def gx_copy(i, o):
        return remote(g_send.at[i, o], g_got.at[i, o], sem_gx, (i, o), dev_8(o))

    def lx_copy(i, o):
        return remote(l_send.at[i, o], l_got.at[i, o], sem_lx, (i, o), dev_8(o))

    def exchange(i, source, send, got, copy):
        both = source[pl.ds(2 * i, 2)].reshape(2 * toks, lat)
        rows = dot(pick[i], both).astype(BF).reshape(g8, 2 * cap, lat)
        got[i, 0] = rows[0]
        send[i] = rows
        for o in range(1, g8):
            copy(i, o).start()

    def pick_grad(i):
        wait_y(m_copy, i)
        wait_y(g_copy, i)
        zero = jnp.zeros((cap, toks), F32)
        weighted = []
        for o in range(g8):
            parts = []
            for s in range(2):
                ranks = meta[1, 2 * i + s, o : o + 1, :]
                parts.append(jnp.where(ranks == place, 1.0, 0.0))
            block = jnp.concatenate(
                [
                    jnp.concatenate([parts[0], zero], axis=1),
                    jnp.concatenate([zero, parts[1]], axis=1),
                ],
                axis=0,
            )
            pick[i, 2 * cap * o : 2 * cap * (o + 1), :] = block.astype(BF)
            w = jnp.concatenate(
                [meta[1, 2 * i + s, g8 + o : g8 + o + 1, :] for s in range(2)], axis=1
            )
            weighted.append(block * w)
        back[i] = jnp.concatenate(weighted, axis=0).T.astype(BF)
        exchange(i, g_all, g_send, g_got, gx_copy)

    early = pairs // 2
    pl.loop(0, early)(pick_grad)

    for o in range(2, g8, 2):
        share = xor(me8, o, g8)
        d_copy(o, share, o).wait_recv()
        cp = d_copy(o + 1, share, 1)
        cp.start()
        sends.append(cp)
    d_copy(1, xor(me8, 1, g8), 1).wait_recv()
    for o in range(2, g8, 2):
        d_copy(o + 1, xor(me8, o + 1, g8), 1).wait_recv()

    depth = tokens.shape[1]
    tile = min(256, depth)
    blocks = tile // (16 * halves)

    def proj_rows(n):
        return proj[pl.ds(n * blocks, blocks)].reshape(tile, lat)

    def latent_step(n, total):
        return total + dot(tokens[:, pl.ds(pl.multiple_of(n * tile, tile), tile)], proj_rows(n))

    latent = lax.fori_loop(0, depth // tile, latent_step, jnp.zeros((toks, lat), F32))
    l_all[0] = latent.astype(BF)

    def l_copy(o):
        return remote(l_all.at[0], l_all.at[o], sem_l, (o,), dev_y(o))

    for o in range(1, ny):
        cp = l_copy(o)
        cp.start()
        sends.append(cp)

    pl.loop(early, pairs)(pick_grad)

    wide = min(256, hid)
    many = g8 * 2 * cap
    lane_is_row = lax.broadcasted_iota(jnp.int32, (2 * cap, 128), 0) == lax.broadcasted_iota(
        jnp.int32, (2 * cap, 128), 1
    )

    def back_grad(i):
        for o in range(1, g8):
            gx_copy(i, o).wait_recv()

        @pl.loop(0, hid // wide)
        def _(n):
            at = pl.ds(pl.multiple_of(n * wide, wide), wide)
            bg[i, :, at] = nt_dot(g_got[i].reshape(many, lat), down[at, :])

    def dispatch(i):
        wait_y(l_copy, i)
        exchange(i, l_all, l_send, l_got, lx_copy)

    def r_copy(i, o):
        return remote(r_send.at[i, o], r_got.at[i, o], sem_r, (i, o), dev_8(o))

    def v_copy(i, o):
        return remote(v_send.at[i, o], v_got.at[i, o], sem_v, (i, o), dev_8(o))

    def experts(i):
        for o in range(1, g8):
            lx_copy(i, o).wait_recv()
        rows = l_got[i].reshape(many, lat)

        def unit_step(n, carry):
            total, sums = carry
            at = pl.ds(pl.multiple_of(n * wide, wide), wide)
            active = jnp.maximum(dot(rows, up[:, at]), 0.0)
            part = bg[i, :, at] * active
            sums = sums + jnp.sum(part * active, axis=1, keepdims=True)
            return total + nt_dot((2.0 * part).astype(BF), up[:, at]), sums

        total, sums = lax.fori_loop(
            0, hid // wide, unit_step, (jnp.zeros((many, lat), F32), jnp.zeros((many, 1), F32))
        )
        out = total.astype(BF).reshape(g8, 2 * cap, lat)
        r_got[i, 0] = out[0]
        r_send[i] = out
        for o in range(g8):
            column = sums[2 * cap * o : 2 * cap * (o + 1)]
            line = jnp.sum(jnp.where(lane_is_row, column, 0.0), axis=0, keepdims=True)
            line = jnp.broadcast_to(line, (8, 128))
            if o == 0:
                v_got[i, 0] = line
            else:
                v_send[i, o] = line
        for o in range(1, g8):
            r_copy(i, o).start()
            v_copy(i, o).start()

    def p_copy(o):
        return remote(p_send.at[o], p_got.at[o], sem_p, (o,), dev_y(o))

    def q_copy(o):
        return remote(q_send.at[o], q_got.at[o], sem_q, (o,), dev_y(o))

    def combine(i):
        for o in range(1, g8):
            r_copy(i, o).wait_recv()
            v_copy(i, o).wait_recv()
        part = dot(back[i], r_got[i].reshape(many, lat)).astype(BF)
        lines = []
        for o in range(g8):
            column = jnp.sum(
                jnp.where(lane_is_row, v_got[i, o, 0:1, :], 0.0), axis=1, keepdims=True
            )
            block = pick[i, 2 * cap * o : 2 * cap * (o + 1), :].astype(F32)
            lines.append(jnp.sum(block * column, axis=0, keepdims=True))
        sums = jnp.concatenate(lines, axis=0)
        p_send[pl.ds(2 * i, 2)] = part.reshape(2, toks, lat)
        for s in range(2):
            q_send[2 * i + s] = sums[:, s * toks : (s + 1) * toks]

        @pl.when(i > 0)
        def _():
            p_copy(2 * i).start()
            q_copy(2 * i).start()

        p_copy(2 * i + 1).start()
        q_copy(2 * i + 1).start()

    @pl.loop(0, pairs + 2)
    def _(k):
        @pl.when(k < pairs)
        def _():
            back_grad(k)
            dispatch(k)

        @pl.when((k >= 1) & (k < pairs + 1))
        def _():
            experts(k - 1)

        @pl.when(k >= 2)
        def _():
            combine(k - 2)

    total = p_send[0].astype(F32)
    for o in range(1, ny):
        p_copy(o).wait_recv()
        total = total + p_got[o].astype(F32)
    lsum[...] = total.astype(BF)
    side = lat // 2
    far_side = pl.ds(pl.multiple_of((1 - c) * side, side), side)
    my_side = pl.ds(pl.multiple_of(c * side, side), side)
    ls_copy = remote(lsum.at[:, far_side], lsum_far, sem_ls, (0,), dev_8(1))
    ls_copy.start()
    sends.append(ls_copy)

    for o in range(1, ny):
        q_copy(o).wait_recv()
    q_got[0] = q_send[0]
    sums = q_got[...].reshape(ny * g8, toks)
    for k in range(routes_t.shape[0]):
        hit = routes_t[k : k + 1, :] == expert
        weight_grad[k : k + 1, :] = jnp.sum(jnp.where(hit, sums, 0.0), axis=0, keepdims=True)

    ls_copy.wait_recv()
    mine, far = lsum[:, my_side], lsum_far[...]
    pair_sum = jnp.concatenate([mine, far], axis=0)

    @pl.loop(0, depth // tile)
    def _(n):
        at = pl.ds(pl.multiple_of(n * tile, tile), tile)
        part = dot(tok_t[at, :], pair_sum).reshape(blocks, halves, 16, side)
        pg32[pl.ds(n * blocks, blocks)] = part
        pg16[pl.ds(n * blocks, blocks)] = part.astype(BF)

    def x_lane(m8):
        return pl.ds(pl.multiple_of((m8 // NC) % 2 * 128, 128), 128)

    def x_copy(o):
        far8 = xor(me8, 2 * o, g8)
        src = pg16.at[:, far8 // NC // 2, :, x_lane(far8)]
        return remote(src, x_got.at[o], sem_x, (o,), dev_8(2 * o))

    for o in range(1, nx):
        cp = x_copy(o)
        cp.start()
        sends.append(cp)

    @pl.loop(0, depth // tile)
    def _(n):
        at = pl.ds(pl.multiple_of(n * tile, tile), tile)
        input_grad[:, at] = nt_dot(lsum[...], proj_rows(n)).astype(BF)

    total = pg32[:, half, :, x_lane(me8)]
    for o in range(1, nx):
        x_copy(o).wait_recv()
        total = total + x_got[o].astype(F32)
    total = total.reshape(nz, ny, 16, 128)
    s32[...] = total
    s16[...] = total.astype(BF)

    def y_copy(o):
        return remote(s16.at[:, xor(y, o, ny)], y_got.at[o], sem_y, (o,), dev_y(o))

    for o in range(1, ny):
        cp = y_copy(o)
        cp.start()
        sends.append(cp)
    total = s32[:, y]
    for o in range(1, ny):
        y_copy(o).wait_recv()
        total = total + y_got[o].astype(F32)
    t16[...] = total.astype(BF)
    s32[:, 0] = total

    def z_copy(o):
        return remote(t16.at[xor(z, o, nz)], z_got.at[o], sem_z, (o,), dev_z(o))

    for o in range(1, nz):
        cp = z_copy(o)
        cp.start()
        sends.append(cp)
    total = s32[z, 0]
    for o in range(1, nz):
        z_copy(o).wait_recv()
        total = total + z_got[o].astype(F32)
    f_send[...] = total
    f_got[:, pl.ds(lane, 128)] = total

    def f_copy(o, m8):
        _, l = share_of(m8)
        return remote(f_send, f_got.at[:, pl.ds(l, 128)], sem_f, (o,), dev_8(o))

    for o in range(1, 4):
        cp = f_copy(o, me8)
        cp.start()
        sends.append(cp)
    for o in range(1, 4):
        f_copy(o, xor(me8, o, g8)).wait_recv()
    rows = jnp.zeros((4, lat), F32)
    for k in range(4):
        rows = rows + jnp.where(me8 % 4 == k, f_got[4 * k : 4 * k + 4, :], 0.0)
    proj_grad[...] = rows

    for cp in sends:
        cp.wait_send()

    @pl.loop(0, pairs)
    def _(i):
        for o in range(1, g8):
            for copy in (gx_copy, lx_copy, r_copy, v_copy):
                copy(i, o).wait_send()

    for o in range(1, ny):
        p_copy(o).wait_send()
        q_copy(o).wait_send()


def on_device(sizes, tokens, latent_grad, routes, route_weights, down_proj, expert_up, expert_down):
    nz, ny, nx, cap = sizes
    toks, depth = tokens.shape
    top = routes.shape[1]
    lat = latent_grad.shape[1]
    hid = expert_up.shape[2]
    g8, halves, pairs = nx * NC, nx // 2, ny // 2
    many = 2 * cap * g8
    e = lax.axis_index("expert")
    place = jnp.arange(16, dtype=jnp.int32) // 4
    own_rows = jnp.where((place == e % 4)[:, None], jnp.tile(down_proj, (4, 1)), 0).astype(BF)
    vmem = pl.BlockSpec(memory_space=pltpu.VMEM)
    dma = pltpu.SemaphoreType.DMA
    buffers = [
        pltpu.VMEM((nz * ny, halves, 16, lat), BF),
        pltpu.VMEM((4, 16, 128), BF),
        pltpu.VMEM((2, ny, 2 * g8, toks), F32),
        pltpu.VMEM((ny, toks, lat), BF),
        pltpu.VMEM((ny, toks, lat), BF),
        pltpu.VMEM((pairs, many, 2 * toks), BF),
        pltpu.VMEM((pairs, 2 * toks, many), BF),
        pltpu.VMEM((pairs, g8, 2 * cap, lat), BF),
        pltpu.VMEM((pairs, g8, 2 * cap, lat), BF),
        pltpu.VMEM((pairs, g8, 2 * cap, lat), BF),
        pltpu.VMEM((pairs, g8, 2 * cap, lat), BF),
        pltpu.VMEM((pairs, many, hid), F32),
        pltpu.VMEM((pairs, g8, 2 * cap, lat), BF),
        pltpu.VMEM((pairs, g8, 2 * cap, lat), BF),
        pltpu.VMEM((pairs, g8, 8, 128), F32),
        pltpu.VMEM((pairs, g8, 8, 128), F32),
        pltpu.VMEM((ny, toks, lat), BF),
        pltpu.VMEM((ny, toks, lat), BF),
        pltpu.VMEM((ny, g8, toks), F32),
        pltpu.VMEM((ny, g8, toks), F32),
        pltpu.VMEM((toks, depth), BF),
        pltpu.VMEM((depth, 2 * toks), BF),
        pltpu.VMEM((toks, lat), BF),
        pltpu.VMEM((toks, lat // 2), BF),
        pltpu.VMEM((nz * ny, halves, 16, lat // 2), F32),
        pltpu.VMEM((nz * ny, halves, 16, lat // 2), BF),
        pltpu.VMEM((nx, nz * ny, 16, 128), BF),
        pltpu.VMEM((nz, ny, 16, 128), F32),
        pltpu.VMEM((nz, ny, 16, 128), BF),
        pltpu.VMEM((ny, nz, 16, 128), BF),
        pltpu.VMEM((nz, 16, 128), BF),
        pltpu.VMEM((nz, 16, 128), BF),
        pltpu.VMEM((16, 128), F32),
        pltpu.VMEM((16, lat), F32),
    ]
    counts = [
        (4,), (ny,), (nz,), (g8,), (ny,), (ny,), (ny,),
        (pairs, g8), (pairs, g8), (pairs, g8), (pairs, g8), (ny,), (ny,),
        (1,), (1,), (nx,), (ny,), (nz,), (4,),
    ]
    input_grad, proj_grad, weight_grad = pl.pallas_call(
        functools.partial(kernel, sizes),
        out_shape=[
            jax.ShapeDtypeStruct((toks, depth), BF),
            jax.ShapeDtypeStruct((4, lat), F32),
            jax.ShapeDtypeStruct((top, toks), F32),
        ],
        in_specs=[vmem] * 7,
        out_specs=[vmem] * 3,
        scratch_shapes=buffers + [dma((2, *count)) for count in counts],
        compiler_params=pltpu.CompilerParams(
            collective_id=0, has_side_effects=True, vmem_limit_bytes=56 * 1024 * 1024
        ),
    )(
        tokens,
        latent_grad,
        routes.T,
        route_weights.astype(F32).T,
        own_rows,
        expert_up[0],
        expert_down[0],
    )
    return input_grad, proj_grad, weight_grad.T.astype(BF)


def build(mesh, nx, cap):
    nz, experts = mesh.shape["dp"], mesh.shape["expert"]
    sizes = (nz, experts // (nx * NC), nx, cap)
    both = P(("dp", "expert"), None)
    one = P("expert", None, None)
    return jax.shard_map(
        functools.partial(on_device, sizes),
        mesh=mesh,
        in_specs=(both, both, both, both, both, one, one),
        out_specs=(both, both, both),
        check_vma=False,
    )


def solution(mesh):
    return build(mesh, 4, 24)
```

```python
import functools

import jax
import jax.numpy as jnp
from jax import lax
from jax.experimental import pallas as pl
from jax.experimental.pallas import tpu as pltpu
from jax.sharding import PartitionSpec as P

MESH = pl.DeviceIdType.MESH
BF = jnp.bfloat16
F32 = jnp.float32
NC = 2


def xor(a, b, n):
    total, bit = 0, 1
    while bit < n:
        total = total + ((a // bit) % 2 + (b // bit) % 2) % 2 * bit
        bit *= 2
    return total


def nt_dot(a, b):
    return lax.dot_general(a, b, (((1,), (1,)), ((), ())), preferred_element_type=F32)


def dot(a, b):
    return jnp.dot(a, b, preferred_element_type=F32)


def remote(src, dst, sems, at, device):
    return pltpu.make_async_remote_copy(
        src_ref=src,
        dst_ref=dst,
        send_sem=sems.at[(0, *at)],
        recv_sem=sems.at[(1, *at)],
        device_id=device,
        device_id_type=MESH,
    )


def kernel(
    sizes,
    tokens_in, grad, routes_t, weights_t, own_rows, up_in, down_in,
    input_grad, proj_grad, weight_grad,
    tokens, up, down, units, order, proj, latent,
    meta, g_all, l_all, pick, back, g_send, l_send, g_got, l_got, bg,
    r_send, r_got, v_send, v_got, p_send, p_got, q_send, q_got,
    tok_far, tok_t, lsum, lsum_far, pg32, pg16, x_got, s32, s16, y_got, z32, z_got, f_send, f_got,
    sem_in, sem_b, sem_c, sem_d, sem_e, sem_m, sem_g, sem_l, sem_gx, sem_lx, sem_r, sem_v, sem_p,
    sem_q, sem_tok, sem_ls, sem_x, sem_y, sem_z, sem_f,
):
    nz, ny, nx, cap = sizes
    g8 = nx * NC
    pairs = ny // 2
    toks, depth = tokens.shape
    lat = grad.shape[1]
    hid = up.shape[1]
    z = lax.axis_index("dp")
    e = lax.axis_index("expert")
    y = e // g8
    me8 = e % g8
    x, c = me8 // NC, me8 % NC

    def dev_z(o):
        return (xor(z, o, nz), e)

    def dev_y(o):
        return (z, xor(y, o, ny) * g8 + me8)

    def dev_step(d):
        return (z, (y + d + ny) % ny * g8 + me8)

    def dev_8(o):
        return (z, y * g8 + xor(me8, o, g8))

    loads = [
        pltpu.make_async_copy(src, dst, sem_in.at[k])
        for k, (src, dst) in enumerate(((tokens_in, tokens), (down_in, down), (up_in, up)))
    ]
    for cp in loads:
        cp.start()
    barrier = pltpu.get_barrier_semaphore()
    for o in range(1, nz):
        pl.semaphore_signal(barrier, inc=1, device_id=dev_z(o), device_id_type=MESH)
    for o in range(1, ny):
        pl.semaphore_signal(barrier, inc=1, device_id=dev_y(o), device_id_type=MESH)
    for o in range(1, g8):
        pl.semaphore_signal(barrier, inc=1, device_id=dev_8(o), device_id_type=MESH)

    own = own_rows[...].astype(F32)
    quarters = lat // 128
    units[c, x, z, y] = jnp.concatenate(
        [own[:, 128 * k : 128 * (k + 1)] for k in range(quarters)], axis=0
    ).astype(BF)

    row = lax.broadcasted_iota(jnp.int32, (ny * g8, toks), 0)
    slot = row // g8
    away = jnp.where(slot % 2 == 0, slot // 2 + 1, -(slot // 2) - 1)
    away = jnp.where(slot == ny - 2, 0, away)
    expert = ((y + away + ny) % ny) * g8 + ((row % g8) ^ me8)
    named = jnp.zeros((ny * g8, toks), F32)
    weight = jnp.zeros((ny * g8, toks), F32)
    weights = weights_t[...].astype(F32)
    for k in range(routes_t.shape[0]):
        hit = routes_t[k : k + 1, :] == expert
        named = jnp.where(hit, 1.0, named)
        weight = jnp.where(hit, weights[k : k + 1, :], weight)
    earlier = (
        lax.broadcasted_iota(jnp.int32, (toks, toks), 0)
        < lax.broadcasted_iota(jnp.int32, (toks, toks), 1)
    )
    rank = dot(named.astype(BF), jnp.where(earlier, 1.0, 0.0).astype(BF))
    rank = jnp.where(named > 0.5, rank, -1.0)
    meta[0] = jnp.concatenate(
        [rank.reshape(ny, g8, toks), weight.reshape(ny, g8, toks)], axis=1
    )
    meta[1, ny - 2] = meta[0, ny - 2]
    g_all[ny - 2] = grad[...]

    block = NC * nx * 2 * 16
    to = lax.broadcasted_iota(jnp.int32, (block, block), 0)
    rest = to % (block // 4)
    origin = (
        ((rest // 4 % NC) * nx + rest // (4 * NC) % nx) * 2 + rest // (4 * NC * nx)
    ) * 16 + to // (block // 4) * 4 + rest % 4
    hit = origin == lax.broadcasted_iota(jnp.int32, (block, block), 1)
    order[...] = jnp.where(hit, 1.0, 0.0).astype(BF)

    pl.semaphore_wait(barrier, nz + ny + g8 - 3)

    sends = []

    def start(cp):
        cp.start()
        sends.append(cp)

    def b_copy(o, at_y):
        ref = units.at[c, x, z, at_y]
        return remote(ref, ref, sem_b, (o,), dev_y(o))

    def c_copy(o, at_z):
        ref = units.at[c, x, at_z]
        return remote(ref, ref, sem_c, (o,), dev_z(o))

    def d_copy(o, ox, at_x):
        ref = units.at[c, at_x, xor(z, o, nz)]
        return remote(ref, ref, sem_d, (o, ox), dev_8(2 * ox))

    def e_copy(o, ox, at_c):
        ref = units.at[at_c, xor(x, ox, nx), xor(z, o, nz)]
        return remote(ref, ref, sem_e, (o, ox), dev_8(1))

    for o in range(1, ny):
        start(b_copy(o, y))

    def m_even(i):
        return remote(
            meta.at[0, 2 * i], meta.at[1, 2 * i + 1], sem_m, (2 * i + 1,), dev_step(i + 1)
        )

    def m_odd(i):
        to = 2 * i + i // (pairs - 1)
        return remote(meta.at[0, 2 * i + 1], meta.at[1, to], sem_m, (to,), dev_step(-i - 1))

    for i in range(pairs):
        if i < pairs - 1:
            start(m_even(i))
        start(m_odd(i))

    def y_near(rows, sem, s):
        away = (1, -1, 2, -2)[s]
        return remote(rows.at[ny - 2], rows.at[s], sem, (s,), dev_step(-away))

    def y_far(rows, sem, s):
        if s < 6:
            return remote(rows.at[s - 2], rows.at[s], sem, (s,), dev_step((-1, 1)[s - 4]))
        at = pl.ds((7 - s) * (toks // 2), toks // 2)
        return remote(
            rows.at[(2, 3)[s - 6], at], rows.at[7, at], sem, (s,), dev_step((-2, 2)[s - 6])
        )

    def y_start(rows, sem):
        for s in range(4):
            start(y_near(rows, sem, s))

    def y_wait(rows, sem, i):
        @pl.when(i < 2)
        def _():
            for k in range(2):
                @pl.when(i == k)
                def _():
                    y_near(rows, sem, 2 * k).wait_recv()
                    y_near(rows, sem, 2 * k + 1).wait_recv()

        @pl.when(i == 1)
        def _():
            for s in range(4, 8):
                y_far(rows, sem, s).start()

        for k in range(2, 4):
            @pl.when(i == k)
            def _():
                y_far(rows, sem, 2 * k).wait_recv()
                y_far(rows, sem, 2 * k + 1).wait_recv()

    y_start(g_all, sem_g)
    loads[0].wait()
    tok_copy = remote(tokens, tok_far, sem_tok, (0,), dev_8(1))
    start(tok_copy)

    for o in range(1, ny):
        b_copy(o, xor(y, o, ny)).wait_recv()
    for o in range(1, nz):
        start(c_copy(o, z))

    @pl.loop(0, nz)
    def _(o):
        @pl.when(o > 0)
        def _():
            c_copy(o, xor(z, o, nz)).wait_recv()

        for ox in range(1, nx):
            d_copy(o, ox, x).start()
        e_copy(o, 0, c).start()

    tok_copy.wait_recv()
    tile = depth // nz

    @pl.loop(0, nz)
    def _(n):
        at = pl.ds(pl.multiple_of(n * tile, tile), tile)
        both = jnp.concatenate([tokens[:, at], tok_far[:, at]], axis=0)
        tok_t[at, :] = both.astype(F32).T.astype(BF)

    place = lax.broadcasted_iota(jnp.int32, (cap, toks), 0).astype(F32)

    def gx_copy(i, o):
        return remote(g_send.at[i, o], g_got.at[i, o], sem_gx, (i, o), dev_8(o))

    def lx_copy(i, o):
        return remote(l_send.at[i, o], l_got.at[i, o], sem_lx, (i, o), dev_8(o))

    def exchange(i, source, send, got, copy):
        both = source[pl.ds(2 * i, 2)].reshape(2 * toks, lat)
        rows = dot(pick[i], both).astype(BF).reshape(g8, 2 * cap, lat)
        got[i, 0] = rows[0]
        send[i] = rows
        for o in range(1, g8):
            copy(i, o).start()

    def pick_grad(i):
        zero = jnp.zeros((cap, toks), F32)
        weighted = []
        for o in range(g8):
            parts = []
            for s in range(2):
                ranks = meta[1, 2 * i + s, o : o + 1, :]
                parts.append(jnp.where(ranks == place, 1.0, 0.0))
            block = jnp.concatenate(
                [
                    jnp.concatenate([parts[0], zero], axis=1),
                    jnp.concatenate([zero, parts[1]], axis=1),
                ],
                axis=0,
            )
            pick[i, 2 * cap * o : 2 * cap * (o + 1), :] = block.astype(BF)
            w = jnp.concatenate(
                [meta[1, 2 * i + s, g8 + o : g8 + o + 1, :] for s in range(2)], axis=1
            )
            weighted.append(block * w)
        exchange(i, g_all, g_send, g_got, gx_copy)
        back[i] = jnp.concatenate(weighted, axis=0).T.astype(BF)

    for i in range(pairs):
        if i < pairs - 1:
            m_even(i).wait_recv()
        m_odd(i).wait_recv()
    for i in range(2):
        y_wait(g_all, sem_g, i)
    pl.loop(0, 2)(pick_grad)

    latent[...] = jnp.zeros_like(latent)

    @pl.loop(0, nz + 1)
    def _(k):
        @pl.when(k < nz)
        def _():
            for ox in range(1, nx):
                d_copy(k, ox, xor(x, ox, nx)).wait_recv()
                e_copy(k, ox, c).start()

        @pl.when(k > 0)
        def _():
            o = k - 1
            for ox in range(nx):
                e_copy(o, ox, 1 - c).wait_recv()
            at_z = xor(z, o, nz)
            for h in range(ny // 2):
                mixed = units[:, :, at_z, 2 * h : 2 * h + 2].reshape(block, 128)
                ordered = dot(order[...], mixed).astype(BF)
                for q in range(quarters):
                    rows = ordered[block // 4 * q : block // 4 * (q + 1)]
                    proj[at_z, h, :, 128 * q : 128 * (q + 1)] = rows
            at = pl.ds(pl.multiple_of(at_z * tile, tile), tile)
            latent[...] += dot(tokens[:, at], proj[at_z].reshape(tile, lat))

    l_all[ny - 2] = latent[...].astype(BF)
    y_start(l_all, sem_l)

    @pl.loop(2, pairs)
    def _(i):
        y_wait(g_all, sem_g, i)
        pick_grad(i)

    loads[1].wait()
    loads[2].wait()
    wide = min(256, hid)
    many = g8 * 2 * cap
    lane_is_row = lax.broadcasted_iota(jnp.int32, (2 * cap, 128), 0) == lax.broadcasted_iota(
        jnp.int32, (2 * cap, 128), 1
    )

    def back_grad(i):
        for o in range(1, g8):
            gx_copy(i, o).wait_recv()

        @pl.loop(0, hid // wide)
        def _(n):
            at = pl.ds(pl.multiple_of(n * wide, wide), wide)
            bg[i, :, at] = nt_dot(g_got[i].reshape(many, lat), down[at, :])

    def dispatch(i):
        y_wait(l_all, sem_l, i)
        exchange(i, l_all, l_send, l_got, lx_copy)

    def r_copy(i, o):
        return remote(r_send.at[i, o], r_got.at[i, o], sem_r, (i, o), dev_8(o))

    def v_copy(i, o):
        return remote(v_send.at[i, o], v_got.at[i, o], sem_v, (i, o), dev_8(o))

    def experts(i):
        for o in range(1, g8):
            lx_copy(i, o).wait_recv()
        rows = l_got[i].reshape(many, lat)

        def unit_step(n, carry):
            total, sums = carry
            at = pl.ds(pl.multiple_of(n * wide, wide), wide)
            active = jnp.maximum(dot(rows, up[:, at]), 0.0)
            part = bg[i, :, at] * active
            sums = sums + jnp.sum(part * active, axis=1, keepdims=True)
            return total + nt_dot((2.0 * part).astype(BF), up[:, at]), sums

        total, sums = lax.fori_loop(
            0, hid // wide, unit_step, (jnp.zeros((many, lat), F32), jnp.zeros((many, 1), F32))
        )
        out = total.astype(BF).reshape(g8, 2 * cap, lat)
        r_got[i, 0] = out[0]
        r_send[i] = out
        for o in range(1, g8):
            r_copy(i, o).start()
        for o in range(g8):
            column = sums[2 * cap * o : 2 * cap * (o + 1)]
            line = jnp.sum(jnp.where(lane_is_row, column, 0.0), axis=0, keepdims=True)
            line = jnp.broadcast_to(line, (8, 128))
            if o == 0:
                v_got[i, 0] = line
            else:
                v_send[i, o] = line
        for o in range(1, g8):
            v_copy(i, o).start()

    def p_even(i):
        return remote(
            p_send.at[2 * i], p_got.at[2 * i + 1], sem_p, (2 * i + 1,), dev_step(i + 1)
        )

    def p_odd(i):
        to = 2 * i + i // (pairs - 1)
        return remote(p_send.at[2 * i + 1], p_got.at[to], sem_p, (to,), dev_step(-i - 1))

    def q_even(i):
        return remote(
            q_send.at[2 * i], q_got.at[2 * i + 1], sem_q, (2 * i + 1,), dev_step(i + 1)
        )

    def q_odd(i):
        to = 2 * i + i // (pairs - 1)
        return remote(q_send.at[2 * i + 1], q_got.at[to], sem_q, (to,), dev_step(-i - 1))

    def combine(i):
        for o in range(1, g8):
            r_copy(i, o).wait_recv()
        part = dot(back[i], r_got[i].reshape(many, lat)).astype(BF)
        p_send[pl.ds(2 * i, 2)] = part.reshape(2, toks, lat)

        @pl.when(i < pairs - 1)
        def _():
            p_even(i).start()

        p_odd(i).start()
        for o in range(1, g8):
            v_copy(i, o).wait_recv()
        lines = []
        for o in range(g8):
            column = jnp.sum(
                jnp.where(lane_is_row, v_got[i, o, 0:1, :], 0.0), axis=1, keepdims=True
            )
            block = pick[i, 2 * cap * o : 2 * cap * (o + 1), :].astype(F32)
            lines.append(jnp.sum(block * column, axis=0, keepdims=True))
        sums = jnp.concatenate(lines, axis=0)
        for s in range(2):
            q_send[2 * i + s] = sums[:, s * toks : (s + 1) * toks]

        @pl.when(i < pairs - 1)
        def _():
            q_even(i).start()

        q_odd(i).start()

    @pl.loop(0, pairs + 2)
    def _(k):
        @pl.when(k < pairs)
        def _():
            dispatch(k)
            back_grad(k)

        @pl.when((k >= 1) & (k < pairs + 1))
        def _():
            experts(k - 1)

        @pl.when(k >= 2)
        def _():
            combine(k - 2)

    total = p_send[ny - 2].astype(F32)
    for i in range(pairs):
        if i < pairs - 1:
            p_even(i).wait_recv()
            total = total + p_got[2 * i + 1].astype(F32)
        p_odd(i).wait_recv()
        total = total + p_got[2 * i + i // (pairs - 1)].astype(F32)
    lsum[...] = total.astype(BF)
    side = lat // 2
    far_side = pl.ds(pl.multiple_of((1 - c) * side, side), side)
    my_side = pl.ds(pl.multiple_of(c * side, side), side)
    ls_copy = remote(lsum.at[:, far_side], lsum_far, sem_ls, (0,), dev_8(1))
    start(ls_copy)

    @pl.loop(0, nz)
    def _(n):
        at = pl.ds(pl.multiple_of(n * tile, tile), tile)
        input_grad[:, at] = nt_dot(lsum[...], proj[n].reshape(tile, lat)).astype(BF)

    ls_copy.wait_recv()
    pair_sum = jnp.concatenate([lsum[:, my_side], lsum_far[...]], axis=0)

    def x_copy(n, ox):
        src = pg16.at[n, xor(x, ox, nx)]
        return remote(src, x_got.at[ox, n], sem_x, (n, ox), dev_8(2 * ox))

    @pl.loop(0, nz)
    def _(n):
        at = pl.ds(pl.multiple_of(n * tile, tile), tile)
        part = dot(tok_t[at, :], pair_sum).reshape(ny, nx, 8, side)
        for k in range(nx):
            piece = part[:, k].reshape(ny * 8, side)
            pg32[n, k] = piece
            pg16[n, k] = piece.astype(BF)
        for ox in range(1, nx):
            x_copy(n, ox).start()

    for i in range(pairs):
        if i < pairs - 1:
            q_even(i).wait_recv()
        q_odd(i).wait_recv()
    q_got[ny - 2] = q_send[ny - 2]
    sums = q_got[...].reshape(ny * g8, toks)
    lines = []
    for k in range(routes_t.shape[0]):
        hit = routes_t[k : k + 1, :] == expert
        lines.append(jnp.sum(jnp.where(hit, sums, 0.0), axis=0, keepdims=True))
    weight_grad[...] = jnp.concatenate(lines, axis=0).astype(BF)

    def y_copy(p, o):
        src = s16.at[p, xor(y, o, ny)]
        return remote(src, y_got.at[o, p], sem_y, (p, o), dev_y(o))

    @pl.loop(0, nz // 2)
    def _(p):
        halves = []
        for s in range(2):
            n = 2 * p + s
            total = pg32[n, x]
            for ox in range(1, nx):
                x_copy(n, ox).wait_recv()
                total = total + x_got[ox, n].astype(F32)
            halves.append(total.reshape(ny, 1, 8, side))
        both = jnp.concatenate(halves, axis=1).reshape(ny, 16, side)
        s32[p] = both
        s16[p] = both.astype(BF)
        for o in range(1, ny):
            y_copy(p, o).start()

    @pl.loop(0, nz // 2)
    def _(p):
        total = s32[p, y]
        for o in range(1, ny):
            y_copy(p, o).wait_recv()
            total = total + y_got[o, p].astype(F32)
        z32[pl.ds(2 * p, 2)] = total.reshape(2, 8, side)

    def z_copy(o):
        return remote(z32.at[xor(z, o, nz)], z_got.at[o], sem_z, (o,), dev_z(o))

    for o in range(1, nz):
        start(z_copy(o))
    total = z32[z]
    for o in range(1, nz):
        z_copy(o).wait_recv()
        total = total + z_got[o]
    f_send[...] = total
    f_copy = remote(f_send, f_got, sem_f, (0,), dev_8(1))
    start(f_copy)
    proj_grad[:, my_side] = jnp.where(c == 0, total[:4], total[4:])
    f_copy.wait_recv()
    proj_grad[:, far_side] = jnp.where(c == 0, f_got[:4, :], f_got[4:, :])

    for cp in sends:
        cp.wait_send()
    for rows, sem in ((g_all, sem_g), (l_all, sem_l)):
        for s in range(4, 8):
            y_far(rows, sem, s).wait_send()

    @pl.loop(0, nz)
    def _(n):
        for ox in range(nx):
            e_copy(n, ox, c).wait_send()
        for ox in range(1, nx):
            d_copy(n, ox, x).wait_send()
            x_copy(n, ox).wait_send()

    @pl.loop(0, nz // 2)
    def _(p):
        for o in range(1, ny):
            y_copy(p, o).wait_send()

    @pl.loop(0, pairs)
    def _(i):
        for o in range(1, g8):
            for copy in (gx_copy, lx_copy, r_copy, v_copy):
                copy(i, o).wait_send()
        p_odd(i).wait_send()
        q_odd(i).wait_send()

        @pl.when(i < pairs - 1)
        def _():
            p_even(i).wait_send()
            q_even(i).wait_send()


def on_device(sizes, tokens, latent_grad, routes, route_weights, down_proj, expert_up, expert_down):
    nz, ny, nx, cap = sizes
    toks, depth = tokens.shape
    top = routes.shape[1]
    lat = latent_grad.shape[1]
    hid = expert_up.shape[2]
    g8, pairs, side = nx * NC, ny // 2, lat // 2
    many = 2 * cap * g8
    block = NC * nx * 2 * 16
    vmem = pl.BlockSpec(memory_space=pltpu.VMEM)
    hbm = pl.BlockSpec(memory_space=pl.ANY)
    dma = pltpu.SemaphoreType.DMA
    buffers = [
        pltpu.VMEM((toks, depth), BF),
        pltpu.VMEM((lat, hid), BF),
        pltpu.VMEM((hid, lat), BF),
        pltpu.VMEM((NC, nx, nz, ny, 16, 128), BF),
        pltpu.VMEM((block, block), BF),
        pltpu.VMEM((nz, ny // 2, block // 4, lat), BF),
        pltpu.VMEM((toks, lat), F32),
        pltpu.VMEM((2, ny, 2 * g8, toks), F32),
        pltpu.VMEM((ny, toks, lat), BF),
        pltpu.VMEM((ny, toks, lat), BF),
        pltpu.VMEM((pairs, many, 2 * toks), BF),
        pltpu.VMEM((pairs, 2 * toks, many), BF),
        pltpu.VMEM((pairs, g8, 2 * cap, lat), BF),
        pltpu.VMEM((pairs, g8, 2 * cap, lat), BF),
        pltpu.VMEM((pairs, g8, 2 * cap, lat), BF),
        pltpu.VMEM((pairs, g8, 2 * cap, lat), BF),
        pltpu.VMEM((pairs, many, hid), F32),
        pltpu.VMEM((pairs, g8, 2 * cap, lat), BF),
        pltpu.VMEM((pairs, g8, 2 * cap, lat), BF),
        pltpu.VMEM((pairs, g8, 8, 128), F32),
        pltpu.VMEM((pairs, g8, 8, 128), F32),
        pltpu.VMEM((ny, toks, lat), BF),
        pltpu.VMEM((ny, toks, lat), BF),
        pltpu.VMEM((ny, g8, toks), F32),
        pltpu.VMEM((ny, g8, toks), F32),
        pltpu.VMEM((toks, depth), BF),
        pltpu.VMEM((depth, 2 * toks), BF),
        pltpu.VMEM((toks, lat), BF),
        pltpu.VMEM((toks, side), BF),
        pltpu.VMEM((nz, nx, ny * 8, side), F32),
        pltpu.VMEM((nz, nx, ny * 8, side), BF),
        pltpu.VMEM((nx, nz, ny * 8, side), BF),
        pltpu.VMEM((nz // 2, ny, 16, side), F32),
        pltpu.VMEM((nz // 2, ny, 16, side), BF),
        pltpu.VMEM((ny, nz // 2, 16, side), BF),
        pltpu.VMEM((nz, 8, side), F32),
        pltpu.VMEM((nz, 8, side), F32),
        pltpu.VMEM((8, side), F32),
        pltpu.VMEM((8, side), F32),
    ]
    counts = [
        (ny,), (nz,), (nz, nx), (nz, nx), (ny,), (ny,), (ny,),
        (pairs, g8), (pairs, g8), (pairs, g8), (pairs, g8), (ny,), (ny,),
        (1,), (1,), (nz, nx), (nz // 2, ny), (nz,), (1,),
    ]
    input_grad, proj_grad, weight_grad = pl.pallas_call(
        functools.partial(kernel, sizes),
        out_shape=[
            jax.ShapeDtypeStruct((toks, depth), BF),
            jax.ShapeDtypeStruct((4, lat), F32),
            jax.ShapeDtypeStruct((top, toks), BF),
        ],
        in_specs=[hbm, vmem, vmem, vmem, vmem, hbm, hbm],
        out_specs=[vmem] * 3,
        scratch_shapes=buffers + [dma((3,))] + [dma((2, *count)) for count in counts],
        compiler_params=pltpu.CompilerParams(
            collective_id=0, has_side_effects=True, vmem_limit_bytes=56 * 1024 * 1024
        ),
    )(
        tokens,
        latent_grad,
        routes.T,
        route_weights.T,
        down_proj,
        expert_up[0],
        expert_down[0],
    )
    return input_grad, proj_grad, weight_grad.T


def build(mesh, nx, cap):
    nz, experts = mesh.shape["dp"], mesh.shape["expert"]
    sizes = (nz, experts // (nx * NC), nx, cap)
    both = P(("dp", "expert"), None)
    one = P("expert", None, None)
    return jax.shard_map(
        functools.partial(on_device, sizes),
        mesh=mesh,
        in_specs=(both, both, both, both, both, one, one),
        out_specs=(both, both, both),
        check_vma=False,
    )


def solution(mesh):
    return build(mesh, 4, 24)
```

```python
import functools

import jax
import jax.numpy as jnp
from jax import lax
from jax.experimental import pallas as pl
from jax.experimental.pallas import tpu as pltpu
from jax.sharding import PartitionSpec as P

MESH = pl.DeviceIdType.MESH
BF = jnp.bfloat16
F32 = jnp.float32
NC = 2


def xor(a, b, n):
    total, bit = 0, 1
    while bit < n:
        total = total + ((a // bit) % 2 + (b // bit) % 2) % 2 * bit
        bit *= 2
    return total


def nt_dot(a, b):
    return lax.dot_general(a, b, (((1,), (1,)), ((), ())), preferred_element_type=F32)


def dot(a, b):
    return jnp.dot(a, b, preferred_element_type=F32)


def remote(src, dst, sems, at, device):
    return pltpu.make_async_remote_copy(
        src_ref=src,
        dst_ref=dst,
        send_sem=sems.at[(0, *at)],
        recv_sem=sems.at[(1, *at)],
        device_id=device,
        device_id_type=MESH,
    )


def kernel(
    sizes,
    tokens_in, grad, routes_t, weights_t, own_rows, up_in, down_in,
    input_grad, proj_grad, weight_grad,
    tokens, up, down, units, order, proj, latent,
    meta, g_all, l_all, pick, back, g_send, l_send, g_got, l_got, bg, pre_grad, grads,
    r_send, r_got, v_send, v_got, p_send, p_got, q_send, q_got,
    tok_far, tok_t, lsum, lsum_far, own_sum, pg32, pg16, x_got, s32, s16, y_got, z32, z_got,
    w32, w16, w_got, u32, u16, u_got,
    sem_in, sem_b, sem_c, sem_d, sem_e, sem_h, sem_i, sem_j, sem_m, sem_g, sem_l, sem_gx, sem_lx, sem_r, sem_v, sem_p,
    sem_q, sem_tok, sem_ls, sem_x, sem_y, sem_z, sem_w, sem_u,
):
    nz, ny, nx, cap = sizes
    g8 = nx * NC
    pairs = ny // 2
    cut = ny * 3 // 4
    toks, depth = tokens.shape
    lat = grad.shape[1]
    hid = up.shape[1]
    z = lax.axis_index("dp")
    e = lax.axis_index("expert")
    y = e // g8
    me8 = e % g8
    x, c = me8 // NC, me8 % NC

    def dev_z(o):
        return (xor(z, o, nz), e)

    def dev_y(o):
        return (z, xor(y, o, ny) * g8 + me8)

    def dev_step(d):
        return (z, (y + d + ny) % ny * g8 + me8)

    def dev_cross(d):
        return (z, (y + d + ny) % ny * g8 + xor(me8, 1, g8))

    def dev_8(o):
        return (z, y * g8 + xor(me8, o, g8))

    loads = [
        pltpu.make_async_copy(src, dst, sem_in.at[k])
        for k, (src, dst) in enumerate(((tokens_in, tokens), (down_in, down), (up_in, up)))
    ]
    for cp in loads:
        cp.start()
    barrier = pltpu.get_barrier_semaphore()
    for o in range(1, nz):
        pl.semaphore_signal(barrier, inc=1, device_id=dev_z(o), device_id_type=MESH)
        other = (xor(z, o, nz), y * g8 + xor(me8, 1, g8))
        pl.semaphore_signal(barrier, inc=1, device_id=other, device_id_type=MESH)
    for o in range(1, ny):
        pl.semaphore_signal(barrier, inc=1, device_id=dev_y(o), device_id_type=MESH)
    for o in range(1, g8):
        pl.semaphore_signal(barrier, inc=1, device_id=dev_8(o), device_id_type=MESH)
    for o in range(1, ny):
        pl.semaphore_signal(barrier, inc=1, device_id=dev_cross(o), device_id_type=MESH)

    own = own_rows[...].astype(F32)
    quarters = lat // 128
    units[c, x, z, y] = jnp.concatenate(
        [own[:, 128 * k : 128 * (k + 1)] for k in range(quarters)], axis=0
    ).astype(BF)

    g_all[ny - 2] = grad[...]
    pl.semaphore_wait(barrier, 2 * (nz + ny) + g8 - 5)

    sends = []

    def start(cp):
        cp.start()
        sends.append(cp)

    def b_copy(o, at_y):
        ref = units.at[c, x, z, at_y]
        return remote(ref, ref, sem_b, (o,), dev_y(o))

    low, high = pl.ds(0, cut), pl.ds(cut, ny - cut)

    def c_copy(o, at_z):
        ref = units.at[c, x, at_z, low]
        return remote(ref, ref, sem_c, (o,), dev_z(o))

    def d_copy(o, ox, at_x):
        ref = units.at[c, at_x, xor(z, o, nz), low]
        return remote(ref, ref, sem_d, (o, ox), dev_8(2 * ox))

    def e_copy(o, ox, at_c):
        ref = units.at[at_c, xor(x, ox, nx), xor(z, o, nz), low]
        return remote(ref, ref, sem_e, (o, ox), dev_8(1))

    def h_copy(ox, at_x):
        ref = units.at[c, at_x, z, high]
        return remote(ref, ref, sem_h, (ox,), dev_8(2 * ox))

    def i_copy(o, at_z):
        ref = units.at[c, :, at_z, high]
        return remote(ref, ref, sem_i, (o,), dev_z(o))

    def j_copy(o, at_c):
        ref = units.at[at_c, :, xor(z, o, nz), high]
        return remote(ref, ref, sem_j, (o,), dev_8(1))

    for o in range(1, ny):
        start(b_copy(o, y))

    def m_even(i):
        return remote(
            meta.at[0, 2 * i], meta.at[1, 2 * i + 1], sem_m, (2 * i + 1,), dev_step(i + 1)
        )

    def m_odd(i):
        to = 2 * i + i // (pairs - 1)
        return remote(meta.at[0, 2 * i + 1], meta.at[1, to], sem_m, (to,), dev_step(-i - 1))

    def y_near(rows, sem, s):
        away = (1, -1, 2, -2)[s]
        return remote(rows.at[ny - 2], rows.at[s], sem, (s,), dev_step(-away))

    def y_far(rows, sem, s):
        if s < 6:
            return remote(rows.at[s - 2], rows.at[s], sem, (s,), dev_step((-1, 1)[s - 4]))
        at = pl.ds((7 - s) * (toks // 2), toks // 2)
        return remote(
            rows.at[(2, 3)[s - 6], at], rows.at[7, at], sem, (s,), dev_step((-2, 2)[s - 6])
        )

    def y_start(rows, sem):
        for s in range(4):
            start(y_near(rows, sem, s))

    def y_wait(rows, sem, i):
        @pl.when(i < 2)
        def _():
            for k in range(2):
                @pl.when(i == k)
                def _():
                    y_near(rows, sem, 2 * k).wait_recv()
                    y_near(rows, sem, 2 * k + 1).wait_recv()

        @pl.when(i == 1)
        def _():
            for s in range(4, 8):
                y_far(rows, sem, s).start()

        for k in range(2, 4):
            @pl.when(i == k)
            def _():
                y_far(rows, sem, 2 * k).wait_recv()
                y_far(rows, sem, 2 * k + 1).wait_recv()

    y_start(g_all, sem_g)

    row = lax.broadcasted_iota(jnp.int32, (ny * g8, toks), 0)
    slot = row // g8
    away = jnp.where(slot % 2 == 0, slot // 2 + 1, -(slot // 2) - 1)
    away = jnp.where(slot == ny - 2, 0, away)
    expert = ((y + away + ny) % ny) * g8 + ((row % g8) ^ me8)
    named = jnp.zeros((ny * g8, toks), F32)
    weight = jnp.zeros((ny * g8, toks), F32)
    weights = weights_t[...].astype(F32)
    for k in range(routes_t.shape[0]):
        hit = routes_t[k : k + 1, :] == expert
        named = jnp.where(hit, 1.0, named)
        weight = jnp.where(hit, weights[k : k + 1, :], weight)
    earlier = (
        lax.broadcasted_iota(jnp.int32, (toks, toks), 0)
        < lax.broadcasted_iota(jnp.int32, (toks, toks), 1)
    )
    rank = dot(named.astype(BF), jnp.where(earlier, 1.0, 0.0).astype(BF))
    rank = jnp.where(named > 0.5, rank, -1.0)
    meta[0] = jnp.concatenate(
        [rank.reshape(ny, g8, toks), weight.reshape(ny, g8, toks)], axis=1
    )
    meta[1, ny - 2] = meta[0, ny - 2]

    block = NC * nx * 2 * 16
    to = lax.broadcasted_iota(jnp.int32, (block, block), 0)
    rest = to % (block // 4)
    origin = (
        ((rest // 4 % NC) * nx + rest // (4 * NC) % nx) * 2 + rest // (4 * NC * nx)
    ) * 16 + to // (block // 4) * 4 + rest % 4
    hit = origin == lax.broadcasted_iota(jnp.int32, (block, block), 1)
    order[...] = jnp.where(hit, 1.0, 0.0).astype(BF)

    for i in range(pairs):
        if i < pairs - 1:
            start(m_even(i))
        start(m_odd(i))

    for o in range(1, ny):
        b_copy(o, xor(y, o, ny)).wait_recv()
    for ox in range(1, nx):
        start(h_copy(ox, x))
    for o in range(1, nz):
        start(c_copy(o, z))
    for ox in range(1, nx):
        h_copy(ox, xor(x, ox, nx)).wait_recv()
    for o in range(1, nz):
        start(i_copy(o, z))

    @pl.loop(0, nz)
    def _(o):
        @pl.when(o > 0)
        def _():
            c_copy(o, xor(z, o, nz)).wait_recv()

        for ox in range(1, nx):
            d_copy(o, ox, x).start()
        e_copy(o, 0, c).start()

    loads[0].wait()
    tok_copy = remote(tokens, tok_far, sem_tok, (0,), dev_8(1))
    start(tok_copy)
    tile = depth // nz

    place = lax.broadcasted_iota(jnp.int32, (cap, toks), 0).astype(F32)

    def gx_copy(i, o):
        return remote(g_send.at[i, o], g_got.at[i, o], sem_gx, (i, o), dev_8(o))

    def lx_copy(i, o):
        return remote(l_send.at[i, o], l_got.at[i, o], sem_lx, (i, o), dev_8(o))

    def exchange(i, source, send, got, copy):
        both = source[pl.ds(2 * i, 2)].reshape(2 * toks, lat)
        rows = dot(pick[i], both).astype(BF).reshape(g8, 2 * cap, lat)
        got[i, 0] = rows[0]
        send[i] = rows
        for o in range(1, g8):
            copy(i, o).start()

    def pick_grad(i):
        zero = jnp.zeros((cap, toks), F32)
        weighted = []
        for o in range(g8):
            parts = []
            for s in range(2):
                ranks = meta[1, 2 * i + s, o : o + 1, :]
                parts.append(jnp.where(ranks == place, 1.0, 0.0))
            block = jnp.concatenate(
                [
                    jnp.concatenate([parts[0], zero], axis=1),
                    jnp.concatenate([zero, parts[1]], axis=1),
                ],
                axis=0,
            )
            pick[i, 2 * cap * o : 2 * cap * (o + 1), :] = block.astype(BF)
            w = jnp.concatenate(
                [meta[1, 2 * i + s, g8 + o : g8 + o + 1, :] for s in range(2)], axis=1
            )
            weighted.append(block * w)
        exchange(i, g_all, g_send, g_got, gx_copy)
        back[i] = jnp.concatenate(weighted, axis=0).T.astype(BF)

    for i in range(pairs):
        if i < pairs - 1:
            m_even(i).wait_recv()
        m_odd(i).wait_recv()
    latent[...] = jnp.zeros_like(latent)

    @pl.loop(0, nz + 1)
    def _(k):
        @pl.when(k < nz)
        def _():
            for ox in range(1, nx):
                d_copy(k, ox, xor(x, ox, nx)).wait_recv()
                e_copy(k, ox, c).start()

            @pl.when(k > 0)
            def _():
                i_copy(k, xor(z, k, nz)).wait_recv()

            j_copy(k, c).start()

        @pl.when(k == nz // 4)
        def _():
            for i in range(2):
                y_wait(g_all, sem_g, i)

        first = nz // 4 + 1

        for i in range(2, pairs):
            @pl.when(k == first + i)
            def _():
                y_wait(g_all, sem_g, i)

        @pl.when((k >= first) & (k < first + pairs))
        def _():
            pick_grad(k - first)

        @pl.when(k > 0)
        def _():
            o = k - 1
            for ox in range(nx):
                e_copy(o, ox, 1 - c).wait_recv()
            j_copy(o, 1 - c).wait_recv()
            at_z = xor(z, o, nz)
            for h in range(ny // 2):
                mixed = units[:, :, at_z, 2 * h : 2 * h + 2].reshape(block, 128)
                ordered = dot(order[...], mixed).astype(BF)
                for q in range(quarters):
                    rows = ordered[block // 4 * q : block // 4 * (q + 1)]
                    proj[at_z, h, :, 128 * q : 128 * (q + 1)] = rows
            at = pl.ds(pl.multiple_of(at_z * tile, tile), tile)
            latent[...] += dot(tokens[:, at], proj[at_z].reshape(tile, lat))

    l_all[ny - 2] = latent[...].astype(BF)
    y_start(l_all, sem_l)

    tok_copy.wait_recv()

    @pl.loop(0, nz)
    def _(n):
        at = pl.ds(pl.multiple_of(n * tile, tile), tile)
        both = jnp.concatenate([tokens[:, at], tok_far[:, at]], axis=0)
        tok_t[at, :] = both.astype(F32).T.astype(BF)

    loads[1].wait()
    loads[2].wait()
    wide = min(256, hid)
    many = g8 * 2 * cap
    lane_is_row = lax.broadcasted_iota(jnp.int32, (2 * cap, 128), 0) == lax.broadcasted_iota(
        jnp.int32, (2 * cap, 128), 1
    )

    def back_grad(i):
        for o in range(1, g8):
            gx_copy(i, o).wait_recv()

        @pl.loop(0, hid // wide)
        def _(n):
            at = pl.ds(pl.multiple_of(n * wide, wide), wide)
            bg[i, :, at] = nt_dot(g_got[i].reshape(many, lat), down[at, :])

    def dispatch(i):
        y_wait(l_all, sem_l, i)
        exchange(i, l_all, l_send, l_got, lx_copy)

    def r_copy(i, o):
        return remote(r_send.at[i, o], r_got.at[i, o], sem_r, (i, o), dev_8(o))

    def v_copy(i, o):
        return remote(v_send.at[i, o], v_got.at[i, o], sem_v, (i, o), dev_8(o))

    def experts(i):
        for o in range(1, g8):
            lx_copy(i, o).wait_recv()
        rows = l_got[i].reshape(many, lat)

        def unit_step(n, sums):
            at = pl.ds(pl.multiple_of(n * wide, wide), wide)
            active = jnp.maximum(dot(rows, up[:, at]), 0.0)
            part = bg[i, :, at] * active
            pre_grad[:, at] = (2.0 * part).astype(BF)
            part = part * active
            for j in range(0, wide, 128):
                sums = sums + part[:, j : j + 128]
            return sums

        sums = lax.fori_loop(0, hid // wide, unit_step, jnp.zeros((many, 128), F32))
        sums = jnp.sum(sums, axis=1, keepdims=True)
        for j in range(0, lat, 256):
            rows = nt_dot(pre_grad[...], up[j : j + 256, :])
            grads[:, j : j + 256] = rows.astype(BF)
        out = grads[...].reshape(g8, 2 * cap, lat)
        r_got[i, 0] = out[0]
        r_send[i] = out
        for o in range(1, g8):
            r_copy(i, o).start()
        for o in range(g8):
            column = sums[2 * cap * o : 2 * cap * (o + 1)]
            line = jnp.sum(jnp.where(lane_is_row, column, 0.0), axis=0, keepdims=True)
            line = jnp.broadcast_to(line, (8, 128))
            if o == 0:
                v_got[i, 0] = line
            else:
                v_send[i, o] = line
        for o in range(1, g8):
            v_copy(i, o).start()

    side = lat // 2

    def p_even(i, far):
        dst = p_got.at[far, 2 * i + 1]
        device = (dev_cross if far else dev_step)(i + 1)
        return remote(p_send.at[far, 2 * i], dst, sem_p, (far, 2 * i + 1), device)

    def p_odd(i, far):
        to = 2 * i + i // (pairs - 1)
        device = (dev_cross if far else dev_step)(-i - 1)
        return remote(p_send.at[far, 2 * i + 1], p_got.at[far, to], sem_p, (far, to), device)

    def p_own():
        return remote(
            p_send.at[1, ny - 2], p_got.at[1, ny - 2], sem_p, (1, ny - 2), dev_8(1)
        )

    def q_even(i):
        return remote(
            q_send.at[2 * i], q_got.at[2 * i + 1], sem_q, (2 * i + 1,), dev_step(i + 1)
        )

    def q_odd(i):
        to = 2 * i + i // (pairs - 1)
        return remote(q_send.at[2 * i + 1], q_got.at[to], sem_q, (to,), dev_step(-i - 1))

    def combine(i):
        for o in range(1, g8):
            r_copy(i, o).wait_recv()
        part = dot(back[i], r_got[i].reshape(many, lat)).astype(BF)
        part = part.reshape(2, toks, lat)
        for h in range(2):
            far = (h + c) % 2
            p_send[far, pl.ds(2 * i, 2)] = part[:, :, side * h : side * (h + 1)]
        for far in range(2):
            p_odd(i, far).start()

            @pl.when(i < pairs - 1)
            def _():
                p_even(i, far).start()

        @pl.when(i == pairs - 1)
        def _():
            p_own().start()

        for o in range(1, g8):
            v_copy(i, o).wait_recv()
        lines = []
        for o in range(g8):
            column = jnp.sum(
                jnp.where(lane_is_row, v_got[i, o, 0:1, :], 0.0), axis=1, keepdims=True
            )
            block = pick[i, 2 * cap * o : 2 * cap * (o + 1), :].astype(F32)
            lines.append(jnp.sum(block * column, axis=0, keepdims=True))
        sums = jnp.concatenate(lines, axis=0)
        for s in range(2):
            q_send[2 * i + s] = sums[:, s * toks : (s + 1) * toks]

        @pl.when(i < pairs - 1)
        def _():
            q_even(i).start()

        q_odd(i).start()

    pl.loop(0, 2)(back_grad)

    @pl.loop(0, pairs + 2)
    def _(k):
        @pl.when(k < pairs)
        def _():
            dispatch(k)

            @pl.when(k == 0)
            def _():
                pl.loop(2, pairs)(back_grad)

        @pl.when((k >= 1) & (k < pairs + 1))
        def _():
            experts(k - 1)

        @pl.when(k >= 2)
        def _():
            combine(k - 2)

    p_own().wait_recv()
    for far in range(2):
        total = (p_got[1, ny - 2] if far else p_send[0, ny - 2]).astype(F32)
        for i in range(pairs):
            if i < pairs - 1:
                p_even(i, far).wait_recv()
                total = total + p_got[far, 2 * i + 1].astype(F32)
            p_odd(i, far).wait_recv()
            total = total + p_got[far, 2 * i + i // (pairs - 1)].astype(F32)
        lsum[toks * far : toks * (far + 1)] = total.astype(BF)
    ls_copy = remote(lsum.at[pl.ds(toks, toks)], lsum_far, sem_ls, (0,), dev_8(1))
    start(ls_copy)

    def x_copy(n, ox):
        src = pg16.at[n, xor(x, ox, nx)]
        return remote(src, x_got.at[ox, n], sem_x, (n, ox), dev_8(2 * ox))

    last = nz // 2 - 1
    for k in range(2):
        part = dot(tok_t[(2 * last + k) * tile : (2 * last + k + 1) * tile, :], lsum[...])
        part = part.reshape(ny, nx * 8, side)
        w32[:, k * nx * 8 : (k + 1) * nx * 8] = part
        w16[:, k * nx * 8 : (k + 1) * nx * 8] = part.astype(BF)

    def w_copy(o):
        return remote(w16.at[xor(y, o, ny)], w_got.at[o], sem_w, (o,), dev_y(o))

    def u_copy(ox):
        return remote(u16.at[xor(x, ox, nx)], u_got.at[ox], sem_u, (ox,), dev_8(2 * ox))

    for o in range(1, ny):
        start(w_copy(o))

    @pl.loop(0, 2 * last)
    def _(n):
        at = pl.ds(pl.multiple_of(n * tile, tile), tile)
        part = dot(tok_t[at, :], lsum[...]).reshape(ny, nx, 8, side)
        for k in range(nx):
            piece = part[:, k].reshape(ny * 8, side)
            pg32[n, k] = piece
            pg16[n, k] = piece.astype(BF)
        for ox in range(1, nx):
            x_copy(n, ox).start()

    ls_copy.wait_recv()
    near, other = lsum[:toks], lsum_far[...]
    own_sum[...] = jnp.concatenate(
        [jnp.where(c == 0, near, other), jnp.where(c == 0, other, near)], axis=1
    )

    @pl.loop(0, nz)
    def _(n):
        at = pl.ds(pl.multiple_of(n * tile, tile), tile)
        input_grad[:, at] = nt_dot(own_sum[...], proj[n].reshape(tile, lat)).astype(BF)

    for i in range(pairs):
        if i < pairs - 1:
            q_even(i).wait_recv()
        q_odd(i).wait_recv()
    q_got[ny - 2] = q_send[ny - 2]
    sums = q_got[...].reshape(ny * g8, toks)
    lines = []
    for k in range(routes_t.shape[0]):
        hit = routes_t[k : k + 1, :] == expert
        lines.append(jnp.sum(jnp.where(hit, sums, 0.0), axis=0, keepdims=True))
    weight_grad[...] = jnp.concatenate(lines, axis=0).astype(BF)

    def y_copy(p, o):
        src = s16.at[p, xor(y, o, ny)]
        return remote(src, y_got.at[o, p], sem_y, (p, o), dev_y(o))

    def x_sum(p):
        halves = []
        for s in range(2):
            n = 2 * p + s
            total = pg32[n, x]
            for ox in range(1, nx):
                x_copy(n, ox).wait_recv()
                total = total + x_got[ox, n].astype(F32)
            halves.append(total.reshape(ny, 1, 8, side))
        both = jnp.concatenate(halves, axis=1).reshape(ny, 16, side)
        s32[p] = both
        s16[p] = both.astype(BF)
        for o in range(1, ny):
            y_copy(p, o).start()

    early = min(2, last)
    pl.loop(0, early)(x_sum)
    total = w32[y]
    for o in range(1, ny):
        w_copy(o).wait_recv()
        total = total + w_got[o].astype(F32)
    total = total.reshape(2, nx, 8, side)
    for k in range(nx):
        piece = total[:, k].reshape(16, side)
        u32[k] = piece
        u16[k] = piece.astype(BF)
    for ox in range(1, nx):
        start(u_copy(ox))
    pl.loop(early, last)(x_sum)

    @pl.loop(0, last)
    def _(p):
        total = s32[p, y]
        for o in range(1, ny):
            y_copy(p, o).wait_recv()
            total = total + y_got[o, p].astype(F32)
        z32[pl.ds(2 * p, 2)] = total.reshape(2, 8, side)

    total = u32[x]
    for ox in range(1, nx):
        u_copy(ox).wait_recv()
        total = total + u_got[ox].astype(F32)
    z32[2 * last : 2 * last + 2] = total.reshape(2, 8, side)

    def z_copy(o, far):
        device = (xor(z, o, nz), y * g8 + xor(me8, far, g8))
        return remote(z32.at[xor(z, o, nz)], z_got.at[far, o], sem_z, (far, o), device)

    for o in range(nz):
        for far in range(0 if o else 1, 2):
            start(z_copy(o, far))
    far_side = pl.ds(pl.multiple_of((1 - c) * side, side), side)
    my_side = pl.ds(pl.multiple_of(c * side, side), side)
    total = z32[z]
    for o in range(1, nz):
        z_copy(o, 0).wait_recv()
        total = total + z_got[0, o]
    proj_grad[:, my_side] = jnp.where(c == 0, total[:4], total[4:])
    z_copy(0, 1).wait_recv()
    total = z_got[1, 0]
    for o in range(1, nz):
        z_copy(o, 1).wait_recv()
        total = total + z_got[1, o]
    proj_grad[:, far_side] = jnp.where(c == 0, total[:4], total[4:])

    for cp in sends:
        cp.wait_send()
    for rows, sem in ((g_all, sem_g), (l_all, sem_l)):
        for s in range(4, 8):
            y_far(rows, sem, s).wait_send()

    p_own().wait_send()

    @pl.loop(0, nz)
    def _(n):
        j_copy(n, c).wait_send()
        for ox in range(nx):
            e_copy(n, ox, c).wait_send()
        for ox in range(1, nx):
            d_copy(n, ox, x).wait_send()

    @pl.loop(0, 2 * last)
    def _(n):
        for ox in range(1, nx):
            x_copy(n, ox).wait_send()

    @pl.loop(0, last)
    def _(p):
        for o in range(1, ny):
            y_copy(p, o).wait_send()

    @pl.loop(0, pairs)
    def _(i):
        for o in range(1, g8):
            for copy in (gx_copy, lx_copy, r_copy, v_copy):
                copy(i, o).wait_send()
        q_odd(i).wait_send()
        for far in range(2):
            p_odd(i, far).wait_send()

        @pl.when(i < pairs - 1)
        def _():
            q_even(i).wait_send()
            for far in range(2):
                p_even(i, far).wait_send()


def on_device(sizes, tokens, latent_grad, routes, route_weights, down_proj, expert_up, expert_down):
    nz, ny, nx, cap = sizes
    toks, depth = tokens.shape
    top = routes.shape[1]
    lat = latent_grad.shape[1]
    hid = expert_up.shape[2]
    g8, pairs, side = nx * NC, ny // 2, lat // 2
    many = 2 * cap * g8
    block = NC * nx * 2 * 16
    vmem = pl.BlockSpec(memory_space=pltpu.VMEM)
    hbm = pl.BlockSpec(memory_space=pl.ANY)
    dma = pltpu.SemaphoreType.DMA
    buffers = [
        pltpu.VMEM((toks, depth), BF),
        pltpu.VMEM((lat, hid), BF),
        pltpu.VMEM((hid, lat), BF),
        pltpu.VMEM((NC, nx, nz, ny, 16, 128), BF),
        pltpu.VMEM((block, block), BF),
        pltpu.VMEM((nz, ny // 2, block // 4, lat), BF),
        pltpu.VMEM((toks, lat), F32),
        pltpu.VMEM((2, ny, 2 * g8, toks), F32),
        pltpu.VMEM((ny, toks, lat), BF),
        pltpu.VMEM((ny, toks, lat), BF),
        pltpu.VMEM((pairs, many, 2 * toks), BF),
        pltpu.VMEM((pairs, 2 * toks, many), BF),
        pltpu.VMEM((pairs, g8, 2 * cap, lat), BF),
        pltpu.VMEM((pairs, g8, 2 * cap, lat), BF),
        pltpu.VMEM((pairs, g8, 2 * cap, lat), BF),
        pltpu.VMEM((pairs, g8, 2 * cap, lat), BF),
        pltpu.VMEM((pairs, many, hid), F32),
        pltpu.VMEM((many, hid), BF),
        pltpu.VMEM((many, lat), BF),
        pltpu.VMEM((pairs, g8, 2 * cap, lat), BF),
        pltpu.VMEM((pairs, g8, 2 * cap, lat), BF),
        pltpu.VMEM((pairs, g8, 8, 128), F32),
        pltpu.VMEM((pairs, g8, 8, 128), F32),
        pltpu.VMEM((2, ny, toks, side), BF),
        pltpu.VMEM((2, ny, toks, side), BF),
        pltpu.VMEM((ny, g8, toks), F32),
        pltpu.VMEM((ny, g8, toks), F32),
        pltpu.VMEM((toks, depth), BF),
        pltpu.VMEM((depth, 2 * toks), BF),
        pltpu.VMEM((2 * toks, side), BF),
        pltpu.VMEM((toks, side), BF),
        pltpu.VMEM((toks, lat), BF),
        pltpu.VMEM((nz, nx, ny * 8, side), F32),
        pltpu.VMEM((nz, nx, ny * 8, side), BF),
        pltpu.VMEM((nx, nz, ny * 8, side), BF),
        pltpu.VMEM((nz // 2, ny, 16, side), F32),
        pltpu.VMEM((nz // 2, ny, 16, side), BF),
        pltpu.VMEM((ny, nz // 2, 16, side), BF),
        pltpu.VMEM((nz, 8, side), F32),
        pltpu.VMEM((2, nz, 8, side), F32),
        pltpu.VMEM((ny, 2 * nx * 8, side), F32),
        pltpu.VMEM((ny, 2 * nx * 8, side), BF),
        pltpu.VMEM((ny, 2 * nx * 8, side), BF),
        pltpu.VMEM((nx, 16, side), F32),
        pltpu.VMEM((nx, 16, side), BF),
        pltpu.VMEM((nx, 16, side), BF),
    ]
    counts = [
        (ny,), (nz,), (nz, nx), (nz, nx), (nx,), (nz,), (nz,), (ny,), (ny,), (ny,),
        (pairs, g8), (pairs, g8), (pairs, g8), (pairs, g8), (2, ny), (ny,),
        (1,), (1,), (nz, nx), (nz // 2, ny), (2, nz), (ny,), (nx,),
    ]
    input_grad, proj_grad, weight_grad = pl.pallas_call(
        functools.partial(kernel, sizes),
        out_shape=[
            jax.ShapeDtypeStruct((toks, depth), BF),
            jax.ShapeDtypeStruct((4, lat), F32),
            jax.ShapeDtypeStruct((top, toks), BF),
        ],
        in_specs=[hbm, vmem, vmem, vmem, vmem, hbm, hbm],
        out_specs=[vmem] * 3,
        scratch_shapes=buffers + [dma((3,))] + [dma((2, *count)) for count in counts],
        compiler_params=pltpu.CompilerParams(
            collective_id=0, has_side_effects=True, vmem_limit_bytes=56 * 1024 * 1024
        ),
    )(
        tokens,
        latent_grad,
        routes.T,
        route_weights.T,
        down_proj,
        expert_up[0],
        expert_down[0],
    )
    return input_grad, proj_grad, weight_grad.T


def build(mesh, nx, cap):
    nz, experts = mesh.shape["dp"], mesh.shape["expert"]
    sizes = (nz, experts // (nx * NC), nx, cap)
    both = P(("dp", "expert"), None)
    one = P("expert", None, None)
    return jax.shard_map(
        functools.partial(on_device, sizes),
        mesh=mesh,
        in_specs=(both, both, both, both, both, one, one),
        out_specs=(both, both, both),
        check_vma=False,
    )


def solution(mesh):
    return build(mesh, 4, 24)
```

```python
import functools

import jax
import jax.numpy as jnp
from jax import lax
from jax.experimental import pallas as pl
from jax.experimental.pallas import tpu as pltpu
from jax.sharding import PartitionSpec as P

MESH = pl.DeviceIdType.MESH
BF = jnp.bfloat16
F32 = jnp.float32
NC = 2


def xor(a, b, n):
    total, bit = 0, 1
    while bit < n:
        total = total + ((a // bit) % 2 + (b // bit) % 2) % 2 * bit
        bit *= 2
    return total


def nt_dot(a, b):
    return lax.dot_general(a, b, (((1,), (1,)), ((), ())), preferred_element_type=F32)


def dot(a, b):
    return jnp.dot(a, b, preferred_element_type=F32)


def remote(src, dst, sems, at, device):
    return pltpu.make_async_remote_copy(
        src_ref=src,
        dst_ref=dst,
        send_sem=sems.at[(0, *at)],
        recv_sem=sems.at[(1, *at)],
        device_id=device,
        device_id_type=MESH,
    )


def kernel(
    sizes,
    tokens_in, grad, routes_t, weights_t, own_rows, up_in, down_in,
    input_grad, proj_grad, weight_grad,
    tokens, up, down, units, order, proj, latent,
    meta, g_all, l_all, pick, back, g_send, l_send, g_got, l_got, bg, pre_grad, grads,
    r_send, r_got, v_send, v_got, p_send, p_got, q_send, q_got,
    tok_far, tok_t, lsum, lsum_far, own_sum, pg32, pg16, x_got, s32, s16, y_got, z32, z_got,
    w32, w16, w_got, u32, u16, u_got,
    sem_in, sem_b, sem_c, sem_d, sem_e, sem_h, sem_i, sem_j, sem_m, sem_g, sem_l, sem_gx, sem_lx, sem_r, sem_v, sem_p,
    sem_q, sem_tok, sem_ls, sem_x, sem_y, sem_z, sem_w, sem_u,
):
    nz, ny, nx, cap = sizes
    g8 = nx * NC
    pairs = ny // 2
    cut = ny * 3 // 4
    toks, depth = tokens.shape
    lat = grad.shape[1]
    hid = up.shape[1]
    z = lax.axis_index("dp")
    e = lax.axis_index("expert")
    y = e // g8
    me8 = e % g8
    x, c = me8 // NC, me8 % NC

    def dev_z(o):
        return (xor(z, o, nz), e)

    def dev_y(o):
        return (z, xor(y, o, ny) * g8 + me8)

    def dev_step(d):
        return (z, (y + d + ny) % ny * g8 + me8)

    def dev_cross(d):
        return (z, (y + d + ny) % ny * g8 + xor(me8, 1, g8))

    def dev_8(o):
        return (z, y * g8 + xor(me8, o, g8))

    loads = [
        pltpu.make_async_copy(src, dst, sem_in.at[k])
        for k, (src, dst) in enumerate(((tokens_in, tokens), (down_in, down), (up_in, up)))
    ]
    for cp in loads:
        cp.start()
    barrier = pltpu.get_barrier_semaphore()
    for o in range(1, nz):
        pl.semaphore_signal(barrier, inc=1, device_id=dev_z(o), device_id_type=MESH)
        other = (xor(z, o, nz), y * g8 + xor(me8, 1, g8))
        pl.semaphore_signal(barrier, inc=1, device_id=other, device_id_type=MESH)
    for o in range(1, ny):
        pl.semaphore_signal(barrier, inc=1, device_id=dev_y(o), device_id_type=MESH)
    for o in range(1, g8):
        pl.semaphore_signal(barrier, inc=1, device_id=dev_8(o), device_id_type=MESH)
    for o in range(1, ny):
        pl.semaphore_signal(barrier, inc=1, device_id=dev_cross(o), device_id_type=MESH)

    own = own_rows[...].astype(F32)
    quarters = lat // 128
    units[c, x, z, y] = jnp.concatenate(
        [own[:, 128 * k : 128 * (k + 1)] for k in range(quarters)], axis=0
    ).astype(BF)

    g_all[ny - 2] = grad[...]
    pl.semaphore_wait(barrier, 2 * (nz + ny) + g8 - 5)

    sends = []

    def start(cp):
        cp.start()
        sends.append(cp)

    def b_copy(o, at_y):
        ref = units.at[c, x, z, at_y]
        return remote(ref, ref, sem_b, (o,), dev_y(o))

    low, high = pl.ds(0, cut), pl.ds(cut, ny - cut)

    def c_copy(o, at_z):
        ref = units.at[c, x, at_z, low]
        return remote(ref, ref, sem_c, (o,), dev_z(o))

    def d_copy(o, ox, at_x):
        ref = units.at[c, at_x, xor(z, o, nz), low]
        return remote(ref, ref, sem_d, (o, ox), dev_8(2 * ox))

    def e_copy(o, ox, at_c):
        ref = units.at[at_c, xor(x, ox, nx), xor(z, o, nz), low]
        return remote(ref, ref, sem_e, (o, ox), dev_8(1))

    def h_copy(ox, at_x):
        ref = units.at[c, at_x, z, high]
        return remote(ref, ref, sem_h, (ox,), dev_8(2 * ox))

    def i_copy(o, at_z):
        ref = units.at[c, :, at_z, high]
        return remote(ref, ref, sem_i, (o,), dev_z(o))

    def j_copy(o, at_c):
        ref = units.at[at_c, :, xor(z, o, nz), high]
        return remote(ref, ref, sem_j, (o,), dev_8(1))

    for o in range(1, ny):
        start(b_copy(o, y))

    def m_even(i):
        return remote(
            meta.at[0, 2 * i], meta.at[1, 2 * i + 1], sem_m, (2 * i + 1,), dev_step(i + 1)
        )

    def m_odd(i):
        to = 2 * i + i // (pairs - 1)
        return remote(meta.at[0, 2 * i + 1], meta.at[1, to], sem_m, (to,), dev_step(-i - 1))

    def y_near(rows, sem, s):
        away = (1, -1, 2, -2)[s]
        return remote(rows.at[ny - 2], rows.at[s], sem, (s,), dev_step(-away))

    def y_far(rows, sem, s):
        if s < 6:
            return remote(rows.at[s - 2], rows.at[s], sem, (s,), dev_step((-1, 1)[s - 4]))
        at = pl.ds((7 - s) * (toks // 2), toks // 2)
        return remote(
            rows.at[(2, 3)[s - 6], at], rows.at[7, at], sem, (s,), dev_step((-2, 2)[s - 6])
        )

    def y_start(rows, sem):
        for s in range(4):
            start(y_near(rows, sem, s))

    def y_wait(rows, sem, i):
        @pl.when(i < 2)
        def _():
            for k in range(2):
                @pl.when(i == k)
                def _():
                    y_near(rows, sem, 2 * k).wait_recv()
                    y_near(rows, sem, 2 * k + 1).wait_recv()

        @pl.when(i == 1)
        def _():
            for s in range(4, 8):
                y_far(rows, sem, s).start()

        for k in range(2, 4):
            @pl.when(i == k)
            def _():
                y_far(rows, sem, 2 * k).wait_recv()
                y_far(rows, sem, 2 * k + 1).wait_recv()

    y_start(g_all, sem_g)

    row = lax.broadcasted_iota(jnp.int32, (ny * g8, toks), 0)
    slot = row // g8
    away = jnp.where(slot % 2 == 0, slot // 2 + 1, -(slot // 2) - 1)
    away = jnp.where(slot == ny - 2, 0, away)
    expert = ((y + away + ny) % ny) * g8 + ((row % g8) ^ me8)
    named = jnp.zeros((ny * g8, toks), F32)
    weight = jnp.zeros((ny * g8, toks), F32)
    weights = weights_t[...].astype(F32)
    for k in range(routes_t.shape[0]):
        hit = routes_t[k : k + 1, :] == expert
        named = jnp.where(hit, 1.0, named)
        weight = jnp.where(hit, weights[k : k + 1, :], weight)
    earlier = (
        lax.broadcasted_iota(jnp.int32, (toks, toks), 0)
        < lax.broadcasted_iota(jnp.int32, (toks, toks), 1)
    )
    rank = dot(named.astype(BF), jnp.where(earlier, 1.0, 0.0).astype(BF))
    rank = jnp.where(named > 0.5, rank, -1.0)
    meta[0] = jnp.concatenate(
        [rank.reshape(ny, g8, toks), weight.reshape(ny, g8, toks)], axis=1
    )
    meta[1, ny - 2] = meta[0, ny - 2]

    block = NC * nx * 2 * 16
    to = lax.broadcasted_iota(jnp.int32, (block, block), 0)
    rest = to % (block // 4)
    origin = (
        ((rest // 4 % NC) * nx + rest // (4 * NC) % nx) * 2 + rest // (4 * NC * nx)
    ) * 16 + to // (block // 4) * 4 + rest % 4
    hit = origin == lax.broadcasted_iota(jnp.int32, (block, block), 1)
    order[...] = jnp.where(hit, 1.0, 0.0).astype(BF)

    for i in range(pairs):
        if i < pairs - 1:
            start(m_even(i))
        start(m_odd(i))

    for o in range(1, ny):
        b_copy(o, xor(y, o, ny)).wait_recv()
    for ox in range(1, nx):
        start(h_copy(ox, x))
    for o in range(1, nz):
        start(c_copy(o, z))
    for ox in range(1, nx):
        h_copy(ox, xor(x, ox, nx)).wait_recv()
    for o in range(1, nz):
        start(i_copy(o, z))

    @pl.loop(0, nz)
    def _(o):
        @pl.when(o > 0)
        def _():
            c_copy(o, xor(z, o, nz)).wait_recv()

        for ox in range(1, nx):
            d_copy(o, ox, x).start()
        e_copy(o, 0, c).start()

    loads[0].wait()
    tok_copy = remote(tokens, tok_far, sem_tok, (0,), dev_8(1))
    start(tok_copy)
    tile = depth // nz

    place = lax.broadcasted_iota(jnp.int32, (cap, toks), 0).astype(F32)

    def gx_copy(i, o):
        return remote(g_send.at[i, o], g_got.at[i, o], sem_gx, (i, o), dev_8(o))

    def lx_copy(i, o):
        return remote(l_send.at[i, o], l_got.at[i, o], sem_lx, (i, o), dev_8(o))

    def exchange(i, source, send, got, copy):
        both = source[pl.ds(2 * i, 2)].reshape(2 * toks, lat)
        rows = dot(pick[i], both).astype(BF).reshape(g8, 2 * cap, lat)
        got[i, 0] = rows[0]
        send[i] = rows
        for o in range(1, g8):
            copy(i, o).start()

    def pick_grad(i):
        zero = jnp.zeros((cap, toks), F32)
        weighted = []
        for o in range(g8):
            parts = []
            for s in range(2):
                ranks = meta[1, 2 * i + s, o : o + 1, :]
                parts.append(jnp.where(ranks == place, 1.0, 0.0))
            block = jnp.concatenate(
                [
                    jnp.concatenate([parts[0], zero], axis=1),
                    jnp.concatenate([zero, parts[1]], axis=1),
                ],
                axis=0,
            )
            pick[i, 2 * cap * o : 2 * cap * (o + 1), :] = block.astype(BF)
            w = jnp.concatenate(
                [meta[1, 2 * i + s, g8 + o : g8 + o + 1, :] for s in range(2)], axis=1
            )
            weighted.append(block * w)
        exchange(i, g_all, g_send, g_got, gx_copy)
        back[i] = jnp.concatenate(weighted, axis=0).T.astype(BF)

    for i in range(pairs):
        if i < pairs - 1:
            m_even(i).wait_recv()
        m_odd(i).wait_recv()
    latent[...] = jnp.zeros_like(latent)

    @pl.loop(0, nz + 1)
    def _(k):
        @pl.when(k < nz)
        def _():
            for ox in range(1, nx):
                d_copy(k, ox, xor(x, ox, nx)).wait_recv()
                e_copy(k, ox, c).start()

            @pl.when(k > 0)
            def _():
                i_copy(k, xor(z, k, nz)).wait_recv()

            j_copy(k, c).start()

        @pl.when(k == nz // 4)
        def _():
            for i in range(2):
                y_wait(g_all, sem_g, i)

        first = nz // 4 + 1

        for i in range(2, pairs):
            @pl.when(k == first + i)
            def _():
                y_wait(g_all, sem_g, i)

        @pl.when((k >= first) & (k < first + pairs))
        def _():
            pick_grad(k - first)

        @pl.when(k > 0)
        def _():
            o = k - 1
            for ox in range(nx):
                e_copy(o, ox, 1 - c).wait_recv()
            j_copy(o, 1 - c).wait_recv()
            at_z = xor(z, o, nz)
            for h in range(ny // 2):
                mixed = units[:, :, at_z, 2 * h : 2 * h + 2].reshape(block, 128)
                ordered = dot(order[...], mixed).astype(BF)
                for q in range(quarters):
                    rows = ordered[block // 4 * q : block // 4 * (q + 1)]
                    proj[at_z, h, :, 128 * q : 128 * (q + 1)] = rows
            at = pl.ds(pl.multiple_of(at_z * tile, tile), tile)
            latent[...] += dot(tokens[:, at], proj[at_z].reshape(tile, lat))

    l_all[ny - 2] = latent[...].astype(BF)
    y_start(l_all, sem_l)

    tok_copy.wait_recv()

    @pl.loop(0, nz)
    def _(n):
        at = pl.ds(pl.multiple_of(n * tile, tile), tile)
        both = jnp.concatenate([tokens[:, at], tok_far[:, at]], axis=0)
        tok_t[at, :] = both.astype(F32).T.astype(BF)

    loads[1].wait()
    loads[2].wait()
    wide = min(256, hid)
    many = g8 * 2 * cap
    lane_is_row = lax.broadcasted_iota(jnp.int32, (2 * cap, 128), 0) == lax.broadcasted_iota(
        jnp.int32, (2 * cap, 128), 1
    )

    def back_grad(i):
        for o in range(1, g8):
            gx_copy(i, o).wait_recv()

        @pl.loop(0, hid // wide)
        def _(n):
            at = pl.ds(pl.multiple_of(n * wide, wide), wide)
            bg[i, :, at] = nt_dot(g_got[i].reshape(many, lat), down[at, :])

    def dispatch(i):
        y_wait(l_all, sem_l, i)
        exchange(i, l_all, l_send, l_got, lx_copy)

    def r_copy(i, o):
        return remote(r_send.at[i, o], r_got.at[i, o], sem_r, (i, o), dev_8(o))

    def v_copy(o):
        return remote(v_send.at[o], v_got.at[o], sem_v, (o,), dev_8(o))

    def experts(i):
        for o in range(1, g8):
            lx_copy(i, o).wait_recv()
        rows = l_got[i].reshape(many, lat)

        def unit_step(n, sums):
            at = pl.ds(pl.multiple_of(n * wide, wide), wide)
            active = jnp.maximum(dot(rows, up[:, at]), 0.0)
            part = bg[i, :, at] * active
            pre_grad[:, at] = (2.0 * part).astype(BF)
            part = part * active
            for j in range(0, wide, 128):
                sums = sums + part[:, j : j + 128]
            return sums

        sums = lax.fori_loop(0, hid // wide, unit_step, jnp.zeros((many, 128), F32))
        sums = jnp.sum(sums, axis=1, keepdims=True)
        for j in range(0, lat, 256):
            rows = nt_dot(pre_grad[...], up[j : j + 256, :])
            grads[:, j : j + 256] = rows.astype(BF)
        out = grads[...].reshape(g8, 2 * cap, lat)
        r_got[i, 0] = out[0]
        r_send[i] = out
        for o in range(1, g8):
            r_copy(i, o).start()
        for o in range(g8):
            column = sums[2 * cap * o : 2 * cap * (o + 1)]
            line = jnp.sum(jnp.where(lane_is_row, column, 0.0), axis=0, keepdims=True)
            v_send[o, pl.ds(i, 1), :] = line

        @pl.when(i == pairs - 1)
        def _():
            for o in range(1, g8):
                v_copy(o).start()

    side = lat // 2

    def p_even(i, far):
        dst = p_got.at[far, 2 * i + 1]
        device = (dev_cross if far else dev_step)(i + 1)
        return remote(p_send.at[far, 2 * i], dst, sem_p, (far, 2 * i + 1), device)

    def p_odd(i, far):
        to = 2 * i + i // (pairs - 1)
        device = (dev_cross if far else dev_step)(-i - 1)
        return remote(p_send.at[far, 2 * i + 1], p_got.at[far, to], sem_p, (far, to), device)

    def p_own():
        return remote(
            p_send.at[1, ny - 2], p_got.at[1, ny - 2], sem_p, (1, ny - 2), dev_8(1)
        )

    def q_even(i):
        return remote(
            q_send.at[2 * i], q_got.at[2 * i + 1], sem_q, (2 * i + 1,), dev_step(i + 1)
        )

    def q_odd(i):
        to = 2 * i + i // (pairs - 1)
        return remote(q_send.at[2 * i + 1], q_got.at[to], sem_q, (to,), dev_step(-i - 1))

    def combine(i):
        for o in range(1, g8):
            r_copy(i, o).wait_recv()
        part = dot(back[i], r_got[i].reshape(many, lat)).astype(BF)
        part = part.reshape(2, toks, lat)
        for h in range(2):
            far = (h + c) % 2
            p_send[far, pl.ds(2 * i, 2)] = part[:, :, side * h : side * (h + 1)]
        for far in range(2):
            p_odd(i, far).start()

            @pl.when(i < pairs - 1)
            def _():
                p_even(i, far).start()

        @pl.when(i == pairs - 1)
        def _():
            p_own().start()

    v_send[...] = jnp.zeros_like(v_send)
    pl.loop(0, 2)(back_grad)

    @pl.loop(0, pairs + 2)
    def _(k):
        @pl.when(k < pairs)
        def _():
            dispatch(k)

            @pl.when(k == 0)
            def _():
                pl.loop(2, pairs)(back_grad)

        @pl.when((k >= 1) & (k < pairs + 1))
        def _():
            experts(k - 1)

        @pl.when(k >= 2)
        def _():
            combine(k - 2)

    v_got[0] = v_send[0]
    for o in range(1, g8):
        v_copy(o).wait_recv()

    @pl.loop(0, pairs)
    def _(i):
        lines = []
        for o in range(g8):
            column = jnp.sum(
                jnp.where(lane_is_row, v_got[o, pl.ds(i, 1), :], 0.0), axis=1, keepdims=True
            )
            block = pick[i, 2 * cap * o : 2 * cap * (o + 1), :].astype(F32)
            lines.append(jnp.sum(block * column, axis=0, keepdims=True))
        sums = jnp.concatenate(lines, axis=0)
        for s in range(2):
            q_send[2 * i + s] = sums[:, s * toks : (s + 1) * toks]

        @pl.when(i < pairs - 1)
        def _():
            q_even(i).start()

        q_odd(i).start()

    p_own().wait_recv()
    for far in range(2):
        total = (p_got[1, ny - 2] if far else p_send[0, ny - 2]).astype(F32)
        for i in range(pairs):
            if i < pairs - 1:
                p_even(i, far).wait_recv()
                total = total + p_got[far, 2 * i + 1].astype(F32)
            p_odd(i, far).wait_recv()
            total = total + p_got[far, 2 * i + i // (pairs - 1)].astype(F32)
        lsum[toks * far : toks * (far + 1)] = total.astype(BF)
    ls_copy = remote(lsum.at[pl.ds(toks, toks)], lsum_far, sem_ls, (0,), dev_8(1))
    start(ls_copy)

    def x_copy(n, ox):
        src = pg16.at[n, xor(x, ox, nx)]
        return remote(src, x_got.at[ox, n], sem_x, (n, ox), dev_8(2 * ox))

    last = nz // 2 - 1
    for k in range(2):
        part = dot(tok_t[(2 * last + k) * tile : (2 * last + k + 1) * tile, :], lsum[...])
        part = part.reshape(ny, nx * 8, side)
        w32[:, k * nx * 8 : (k + 1) * nx * 8] = part
        w16[:, k * nx * 8 : (k + 1) * nx * 8] = part.astype(BF)

    def w_copy(o):
        return remote(w16.at[xor(y, o, ny)], w_got.at[o], sem_w, (o,), dev_y(o))

    def u_copy(ox):
        return remote(u16.at[xor(x, ox, nx)], u_got.at[ox], sem_u, (ox,), dev_8(2 * ox))

    for o in range(1, ny):
        start(w_copy(o))

    @pl.loop(0, 2 * last)
    def _(n):
        at = pl.ds(pl.multiple_of(n * tile, tile), tile)
        part = dot(tok_t[at, :], lsum[...]).reshape(ny, nx, 8, side)
        for k in range(nx):
            piece = part[:, k].reshape(ny * 8, side)
            pg32[n, k] = piece
            pg16[n, k] = piece.astype(BF)
        for ox in range(1, nx):
            x_copy(n, ox).start()

    ls_copy.wait_recv()
    near, other = lsum[:toks], lsum_far[...]
    own_sum[...] = jnp.concatenate(
        [jnp.where(c == 0, near, other), jnp.where(c == 0, other, near)], axis=1
    )

    @pl.loop(0, nz)
    def _(n):
        at = pl.ds(pl.multiple_of(n * tile, tile), tile)
        input_grad[:, at] = nt_dot(own_sum[...], proj[n].reshape(tile, lat)).astype(BF)

    for i in range(pairs):
        if i < pairs - 1:
            q_even(i).wait_recv()
        q_odd(i).wait_recv()
    q_got[ny - 2] = q_send[ny - 2]
    sums = q_got[...].reshape(ny * g8, toks)
    lines = []
    for k in range(routes_t.shape[0]):
        hit = routes_t[k : k + 1, :] == expert
        lines.append(jnp.sum(jnp.where(hit, sums, 0.0), axis=0, keepdims=True))
    weight_grad[...] = jnp.concatenate(lines, axis=0).astype(BF)

    def y_copy(p, o):
        src = s16.at[p, xor(y, o, ny)]
        return remote(src, y_got.at[o, p], sem_y, (p, o), dev_y(o))

    def x_sum(p):
        halves = []
        for s in range(2):
            n = 2 * p + s
            total = pg32[n, x]
            for ox in range(1, nx):
                x_copy(n, ox).wait_recv()
                total = total + x_got[ox, n].astype(F32)
            halves.append(total.reshape(ny, 1, 8, side))
        both = jnp.concatenate(halves, axis=1).reshape(ny, 16, side)
        s32[p] = both
        s16[p] = both.astype(BF)
        for o in range(1, ny):
            y_copy(p, o).start()

    early = min(2, last)
    pl.loop(0, early)(x_sum)
    total = w32[y]
    for o in range(1, ny):
        w_copy(o).wait_recv()
        total = total + w_got[o].astype(F32)
    total = total.reshape(2, nx, 8, side)
    for k in range(nx):
        piece = total[:, k].reshape(16, side)
        u32[k] = piece
        u16[k] = piece.astype(BF)
    for ox in range(1, nx):
        start(u_copy(ox))
    pl.loop(early, last)(x_sum)

    @pl.loop(0, last)
    def _(p):
        total = s32[p, y]
        for o in range(1, ny):
            y_copy(p, o).wait_recv()
            total = total + y_got[o, p].astype(F32)
        z32[pl.ds(2 * p, 2)] = total.reshape(2, 8, side)

    total = u32[x]
    for ox in range(1, nx):
        u_copy(ox).wait_recv()
        total = total + u_got[ox].astype(F32)
    z32[2 * last : 2 * last + 2] = total.reshape(2, 8, side)

    def z_copy(o, far):
        device = (xor(z, o, nz), y * g8 + xor(me8, far, g8))
        return remote(z32.at[xor(z, o, nz)], z_got.at[far, o], sem_z, (far, o), device)

    for o in range(nz):
        for far in range(0 if o else 1, 2):
            start(z_copy(o, far))
    far_side = pl.ds(pl.multiple_of((1 - c) * side, side), side)
    my_side = pl.ds(pl.multiple_of(c * side, side), side)
    total = z32[z]
    for o in range(1, nz):
        z_copy(o, 0).wait_recv()
        total = total + z_got[0, o]
    proj_grad[:, my_side] = jnp.where(c == 0, total[:4], total[4:])
    z_copy(0, 1).wait_recv()
    total = z_got[1, 0]
    for o in range(1, nz):
        z_copy(o, 1).wait_recv()
        total = total + z_got[1, o]
    proj_grad[:, far_side] = jnp.where(c == 0, total[:4], total[4:])

    for cp in sends:
        cp.wait_send()
    for rows, sem in ((g_all, sem_g), (l_all, sem_l)):
        for s in range(4, 8):
            y_far(rows, sem, s).wait_send()

    p_own().wait_send()
    for o in range(1, g8):
        v_copy(o).wait_send()

    @pl.loop(0, nz)
    def _(n):
        j_copy(n, c).wait_send()
        for ox in range(nx):
            e_copy(n, ox, c).wait_send()
        for ox in range(1, nx):
            d_copy(n, ox, x).wait_send()

    @pl.loop(0, 2 * last)
    def _(n):
        for ox in range(1, nx):
            x_copy(n, ox).wait_send()

    @pl.loop(0, last)
    def _(p):
        for o in range(1, ny):
            y_copy(p, o).wait_send()

    @pl.loop(0, pairs)
    def _(i):
        for o in range(1, g8):
            for copy in (gx_copy, lx_copy, r_copy):
                copy(i, o).wait_send()
        q_odd(i).wait_send()
        for far in range(2):
            p_odd(i, far).wait_send()

        @pl.when(i < pairs - 1)
        def _():
            q_even(i).wait_send()
            for far in range(2):
                p_even(i, far).wait_send()


def on_device(sizes, tokens, latent_grad, routes, route_weights, down_proj, expert_up, expert_down):
    nz, ny, nx, cap = sizes
    toks, depth = tokens.shape
    top = routes.shape[1]
    lat = latent_grad.shape[1]
    hid = expert_up.shape[2]
    g8, pairs, side = nx * NC, ny // 2, lat // 2
    many = 2 * cap * g8
    block = NC * nx * 2 * 16
    vmem = pl.BlockSpec(memory_space=pltpu.VMEM)
    hbm = pl.BlockSpec(memory_space=pl.ANY)
    dma = pltpu.SemaphoreType.DMA
    buffers = [
        pltpu.VMEM((toks, depth), BF),
        pltpu.VMEM((lat, hid), BF),
        pltpu.VMEM((hid, lat), BF),
        pltpu.VMEM((NC, nx, nz, ny, 16, 128), BF),
        pltpu.VMEM((block, block), BF),
        pltpu.VMEM((nz, ny // 2, block // 4, lat), BF),
        pltpu.VMEM((toks, lat), F32),
        pltpu.VMEM((2, ny, 2 * g8, toks), F32),
        pltpu.VMEM((ny, toks, lat), BF),
        pltpu.VMEM((ny, toks, lat), BF),
        pltpu.VMEM((pairs, many, 2 * toks), BF),
        pltpu.VMEM((pairs, 2 * toks, many), BF),
        pltpu.VMEM((pairs, g8, 2 * cap, lat), BF),
        pltpu.VMEM((pairs, g8, 2 * cap, lat), BF),
        pltpu.VMEM((pairs, g8, 2 * cap, lat), BF),
        pltpu.VMEM((pairs, g8, 2 * cap, lat), BF),
        pltpu.VMEM((pairs, many, hid), F32),
        pltpu.VMEM((many, hid), BF),
        pltpu.VMEM((many, lat), BF),
        pltpu.VMEM((pairs, g8, 2 * cap, lat), BF),
        pltpu.VMEM((pairs, g8, 2 * cap, lat), BF),
        pltpu.VMEM((g8, 8, 128), F32),
        pltpu.VMEM((g8, 8, 128), F32),
        pltpu.VMEM((2, ny, toks, side), BF),
        pltpu.VMEM((2, ny, toks, side), BF),
        pltpu.VMEM((ny, g8, toks), F32),
        pltpu.VMEM((ny, g8, toks), F32),
        pltpu.VMEM((toks, depth), BF),
        pltpu.VMEM((depth, 2 * toks), BF),
        pltpu.VMEM((2 * toks, side), BF),
        pltpu.VMEM((toks, side), BF),
        pltpu.VMEM((toks, lat), BF),
        pltpu.VMEM((nz, nx, ny * 8, side), F32),
        pltpu.VMEM((nz, nx, ny * 8, side), BF),
        pltpu.VMEM((nx, nz, ny * 8, side), BF),
        pltpu.VMEM((nz // 2, ny, 16, side), F32),
        pltpu.VMEM((nz // 2, ny, 16, side), BF),
        pltpu.VMEM((ny, nz // 2, 16, side), BF),
        pltpu.VMEM((nz, 8, side), F32),
        pltpu.VMEM((2, nz, 8, side), F32),
        pltpu.VMEM((ny, 2 * nx * 8, side), F32),
        pltpu.VMEM((ny, 2 * nx * 8, side), BF),
        pltpu.VMEM((ny, 2 * nx * 8, side), BF),
        pltpu.VMEM((nx, 16, side), F32),
        pltpu.VMEM((nx, 16, side), BF),
        pltpu.VMEM((nx, 16, side), BF),
    ]
    counts = [
        (ny,), (nz,), (nz, nx), (nz, nx), (nx,), (nz,), (nz,), (ny,), (ny,), (ny,),
        (pairs, g8), (pairs, g8), (pairs, g8), (g8,), (2, ny), (ny,),
        (1,), (1,), (nz, nx), (nz // 2, ny), (2, nz), (ny,), (nx,),
    ]
    input_grad, proj_grad, weight_grad = pl.pallas_call(
        functools.partial(kernel, sizes),
        out_shape=[
            jax.ShapeDtypeStruct((toks, depth), BF),
            jax.ShapeDtypeStruct((4, lat), F32),
            jax.ShapeDtypeStruct((top, toks), BF),
        ],
        in_specs=[hbm, vmem, vmem, vmem, vmem, hbm, hbm],
        out_specs=[vmem] * 3,
        scratch_shapes=buffers + [dma((3,))] + [dma((2, *count)) for count in counts],
        compiler_params=pltpu.CompilerParams(
            collective_id=0, has_side_effects=True, vmem_limit_bytes=56 * 1024 * 1024
        ),
    )(
        tokens,
        latent_grad,
        routes.T,
        route_weights.T,
        down_proj,
        expert_up[0],
        expert_down[0],
    )
    return input_grad, proj_grad, weight_grad.T


def build(mesh, nx, cap):
    nz, experts = mesh.shape["dp"], mesh.shape["expert"]
    sizes = (nz, experts // (nx * NC), nx, cap)
    both = P(("dp", "expert"), None)
    one = P("expert", None, None)
    return jax.shard_map(
        functools.partial(on_device, sizes),
        mesh=mesh,
        in_specs=(both, both, both, both, both, one, one),
        out_specs=(both, both, both),
        check_vma=False,
    )


def solution(mesh):
    return build(mesh, 4, 24)
```
